32 devices in a mesh: wide: 16 (over z, y, core), narrow: 2 (over x).
Axes of the slice: x: 2, y: 2, z: 4, core: 2. Of those that a mesh axis runs over, the one named last changes fastest.
Arguments:
- key_grads: bfloat16 [16, 2, 2, 2048, 512], P('wide', 'narrow'), may hold values from -1600 to 1600
- router_grads: bfloat16 [16, 2, 2, 64, 2048], P('wide', 'narrow'), may hold values from -1600 to 1600
- gain_grads: bfloat16 [16, 2, 2, 2048], P('wide', 'narrow'), may hold values from -1600 to 1600
- key_master: float32 [2048, 512], P('narrow'), may hold values from -3 to 3
- key_first: float32 [2048, 512], P('narrow'), may hold values from -3 to 3
- key_second: float32 [2048, 512], P('narrow'), may hold values from 0.01 to 1
- router_master: float32 [64, 2048], P(None, 'narrow'), may hold values from -3 to 3
- router_first: float32 [64, 2048], P(None, 'narrow'), may hold values from -3 to 3
- router_second: float32 [64, 2048], P(None, 'narrow'), may hold values from 0.01 to 1
- gain_master: float32 [2048], P('narrow'), may hold values from 0.5 to 1.5
- gain_first: float32 [2048], P('narrow'), may hold values from -3 to 3
- gain_second: float32 [2048], P('narrow'), may hold values from 0.01 to 1
Outputs:
- key_master_new: float32 [2048, 512], P('narrow')
- key_first_new: float32 [2048, 512], P('narrow')
- key_second_new: float32 [2048, 512], P('narrow')
- router_master_new: float32 [64, 2048], P(None, 'narrow')
- router_first_new: float32 [64, 2048], P(None, 'narrow')
- router_second_new: float32 [64, 2048], P(None, 'narrow')
- gain_master_new: float32 [2048], P('narrow')
- gain_first_new: float32 [2048], P('narrow')
- gain_second_new: float32 [2048], P('narrow')
- key_weight: bfloat16 [2048, 512], replicated
- router_weight: bfloat16 [64, 2048], replicated
- gain_weight: bfloat16 [2048], replicated
The draws below stay inside these ranges and needn't reach their ends.
All inputs are finite; a program needn't handle non-finite values.
Results may differ from the reference program's by a relative error of at most 0.002.
Values may be sent and summed in bfloat16 or wider, within the bound.
A program may use at most 64 MiB of HBM per device.

```python
import math
import jax
import jax.numpy as jnp
from jax import lax

D = 2048
KEY_WIDTH = 512
EXPERTS = 64
MICRO = 2
N_WIDE = 16
N_NARROW = 2


def scaled_grads(key, leading, row_count, col_count, rows_last):
    streams = jax.random.split(key, 3)
    row_place = jnp.arange(row_count, dtype=jnp.float32) / row_count
    row_scale = jnp.exp(jax.random.uniform(streams[1], (row_count,)) * math.log(10.0)) * jnp.exp(row_place * math.log(3.0))
    col_scale = jnp.exp(jax.random.uniform(streams[2], (col_count,)) * math.log(10.0))
    if rows_last:
        trailing = (col_count, row_count)
        surface = col_scale[:, None] * row_scale[None, :]
    else:
        trailing = (row_count, col_count)
        surface = row_scale[:, None] * col_scale[None, :]
    values = jax.random.truncated_normal(streams[0], -4.0, 4.0, leading + trailing)
    return (0.3 * values * surface).astype(jnp.float32)


def draw_key_grads(key, part):
    return scaled_grads(jax.random.fold_in(key, 11), (N_WIDE, N_NARROW, MICRO), D, KEY_WIDTH, False).astype(jnp.bfloat16)


def draw_router_grads(key, part):
    return scaled_grads(jax.random.fold_in(key, 12), (N_WIDE, N_NARROW, MICRO), D, EXPERTS, True).astype(jnp.bfloat16)


def draw_gain_grads(key, part):
    produced = scaled_grads(jax.random.fold_in(key, 13), (N_WIDE, N_NARROW, MICRO), D, 1, False)
    return produced.reshape((N_WIDE, N_NARROW, MICRO, D)).astype(jnp.bfloat16)


def shard_levels(own_key, extent, shards, least, top_value):
    factor_of, own = 1.0, jax.random.fold_in(own_key, 6)
    for axis_at, blocks in shards:
        heights = jnp.exp(jax.random.uniform(jax.random.fold_in(own, axis_at), (blocks,), jnp.float32, least / len(shards), top_value / len(shards)))
        factor_of = factor_of * jnp.repeat(heights, extent[axis_at] // blocks).reshape([-1 if axis == axis_at else 1 for axis in range(len(extent))])
    return factor_of


def noise(rng, extent, scale, most, cuts=(), kind=jnp.bfloat16):
    drawn = jax.random.normal(rng, extent, jnp.float32) * scale
    if len(cuts) > 0:
        drawn = shard_levels(rng, extent, cuts, -0.22, 0.18) * drawn
    return jnp.clip(drawn, min=-most, max=most).astype(kind)


def setup_inputs(seed: int = 0) -> dict:
    key_list = jax.random.split(jax.random.key(seed), 13)
    key_grads = draw_key_grads(jax.random.fold_in(key_list[12], 71), 0)
    router_grads = draw_router_grads(jax.random.fold_in(key_list[12], 71), 0)
    gain_grads = draw_gain_grads(jax.random.fold_in(key_list[12], 71), 0)
    key_master = noise(key_list[3], (D, KEY_WIDTH), 0.5, 3.0, ((0, 2),), jnp.float32)
    key_first = noise(key_list[4], (D, KEY_WIDTH), 0.3, 3.0, ((0, 2),), jnp.float32)
    key_second = jnp.clip(jnp.exp(math.log(1.0) - 4.6051702 * jax.random.uniform(key_list[5], (D, KEY_WIDTH), jnp.float32) ** shard_levels(key_list[5], (D, KEY_WIDTH), ((0, 2),), -0.2, 0.2)), 0.01, 1.0)
    router_master = noise(key_list[6], (EXPERTS, D), 0.5, 3.0, ((1, 2),), jnp.float32)
    router_first = noise(key_list[7], (EXPERTS, D), 0.3, 3.0, ((1, 2),), jnp.float32)
    router_second = jnp.clip(jnp.exp(math.log(1.0) - 4.6051702 * jax.random.uniform(key_list[8], (EXPERTS, D), jnp.float32) ** shard_levels(key_list[8], (EXPERTS, D), ((1, 2),), -0.2, 0.2)), 0.01, 1.0)
    gain_master = jnp.clip(0.5 + 1.0 * jax.random.uniform(key_list[9], (D,), jnp.float32) ** shard_levels(key_list[9], (D,), ((0, 2),), -0.2, 0.2), 0.5, 1.5)
    gain_first = noise(key_list[10], (D,), 0.3, 3.0, ((0, 2),), jnp.float32)
    gain_second = jnp.clip(jnp.exp(math.log(1.0) - 4.6051702 * jax.random.uniform(key_list[11], (D,), jnp.float32) ** shard_levels(key_list[11], (D,), ((0, 2),), -0.2, 0.2)), 0.01, 1.0)
    return dict(key_grads=key_grads, router_grads=router_grads, gain_grads=gain_grads, key_master=key_master, key_first=key_first, key_second=key_second, router_master=router_master, router_first=router_first, router_second=router_second, gain_master=gain_master, gain_first=gain_first, gain_second=gain_second)


beta_one = 0.9
beta_two = 0.95
step_rate = 0.01
epsilon = 1e-08
bias_one = 1.0 - 0.9 ** 10
bias_two = 1.0 - 0.95 ** 10

def reduce_grads(grad_stack):

    def accumulate(summed, blocks):
        locals_sum = lax.optimization_barrier(jnp.sum(blocks.astype(jnp.float32), axis=1)).astype(jnp.bfloat16)
        return (summed + lax.optimization_barrier(jnp.sum(locals_sum.astype(jnp.float32), axis=0)), None)
    start_value = jnp.zeros(grad_stack.shape[3:], jnp.float32)
    summed, unused = lax.scan(accumulate, start_value, grad_stack)
    return summed

def adamw(master, first_moment, second, gradient, factor, decay_rate):
    scaled = factor * gradient
    first_new = beta_one * first_moment + (1.0 - beta_one) * scaled
    second_new = beta_two * second + (1.0 - beta_two) * scaled * scaled
    update = first_new / bias_one / (jnp.sqrt(second_new / bias_two) + epsilon) + decay_rate * master
    master_new = master - step_rate * update
    return (master_new, first_new, second_new)

def reference(key_grads, router_grads, gain_grads, key_master, key_first, key_second, router_master, router_first, router_second, gain_master, gain_first, gain_second):
    grad_key = reduce_grads(key_grads)
    grad_router = reduce_grads(router_grads)
    grad_gain = reduce_grads(gain_grads)
    totals = jnp.sum(grad_key * grad_key) + jnp.sum(grad_router * grad_router) + jnp.sum(grad_gain * grad_gain)
    clip_limit = 0.5 * math.sqrt(D * KEY_WIDTH + EXPERTS * D + D)
    factor = clip_limit / jnp.maximum(jnp.sqrt(totals), clip_limit)
    key_new, key_first_new, key_second_new = adamw(key_master, key_first, key_second, grad_key, factor, 0.1)
    router_new, router_first_new, router_second_new = adamw(router_master, router_first, router_second, grad_router, factor, 0.1)
    gain_new, gain_first_new, gain_second_new = adamw(gain_master, gain_first, gain_second, grad_gain, factor, 0.0)
    return (key_new, key_first_new, key_second_new, router_new, router_first_new, router_second_new, gain_new, gain_first_new, gain_second_new, key_new.astype(jnp.bfloat16), router_new.astype(jnp.bfloat16), gain_new.astype(jnp.bfloat16))
```

```python
import functools
import math

import jax
import jax.numpy as jnp
from jax import lax
from jax.experimental import pallas as pl
from jax.experimental.pallas import tpu as pltpu
from jax.sharding import PartitionSpec as P

beta_one = 0.9
beta_two = 0.95
step_rate = 0.01
epsilon = 1e-08
bias_one = 1.0 - 0.9**10
bias_two = 1.0 - 0.95**10

LANES = 256
PARTS = 3
HALVED_BITS = 4
F32, BF16 = jnp.float32, jnp.bfloat16


def adamw(master, first_moment, second, gradient, factor, decay_rate):
    scaled = factor * gradient
    first_new = beta_one * first_moment + (1.0 - beta_one) * scaled
    second_new = beta_two * second + (1.0 - beta_two) * scaled * scaled
    update = (
        first_new / bias_one / (jnp.sqrt(second_new / bias_two) + epsilon) + decay_rate * master
    )
    master_new = master - step_rate * update
    return (master_new, first_new, second_new)


def rows_loop(count, step, body):
    def one(i, carry):
        body(pl.multiple_of(i * step, 16))
        return carry

    lax.fori_loop(0, count // step, one, 0)


def layout(key_shape, router_shape):
    half_rows, half_cols = key_shape[0] // 2, router_shape[1] // 2
    blocks, at = [], 0
    for col in range(0, key_shape[1], LANES):
        blocks.append((at, half_rows, "key", col))
        at += half_rows
    for col in range(0, half_cols, LANES):
        blocks.append((at, router_shape[0], "router", col))
        at += router_shape[0]
    return blocks, at


def part_orders():
    return (("x", 1, 2), (1, 2, "x"), (2, "x", 1))


def stage_shapes(part_rows, wide_bits):
    plans = []
    for order in part_orders():
        halves, count, plan = 2, part_rows, []
        for axis in (0,) + order + (3,):
            if axis == "x":
                halves = 1
            else:
                count //= 2
            plan.append((axis, (halves, count, LANES)))
        for axis in range(HALVED_BITS, wide_bits):
            plan.append((axis, (halves, count, LANES)))
        plans.append(plan)
    return plans


def reduce_kernel(
    plans,
    blocks,
    total_rows,
    clip_limit,
    key_ref,
    router_ref,
    gain_ref,
    key_out,
    router_out,
    gain_out,
    factor_out,
    local,
    acc,
    full,
    gain_val,
    gain_in,
    square_val,
    square_in,
    send_bufs,
    recv_bufs,
    send_sem,
    recv_sem,
    gather_send,
    gather_recv,
    gain_send,
    gain_recv,
    square_send,
    square_recv,
):
    wide, narrow = lax.axis_index("wide"), lax.axis_index("narrow")
    stages = len(plans[0])
    part_rows = total_rows // PARTS
    wide_bits = stages - 1
    bit = [(wide // 2**k) % 2 for k in range(wide_bits)]

    def partner(axis):
        if axis == "x":
            return (wide, 1 - narrow)
        return (wide + (1 - 2 * bit[axis]) * 2**axis, narrow)

    diagonal = (partner(3)[0], 1 - narrow)
    friends = [partner(a) for a in ["x"] + list(range(wide_bits))] + [diagonal]
    barrier = pltpu.get_barrier_semaphore()
    for friend in friends:
        pl.semaphore_signal(barrier, inc=1, device_id=friend, device_id_type=pl.DeviceIdType.MESH)
    pl.semaphore_wait(barrier, len(friends))

    def remote(src, dst, send, recv, to):
        return pltpu.make_async_remote_copy(
            src_ref=src,
            dst_ref=dst,
            send_sem=send,
            recv_sem=recv,
            device_id=to,
            device_id_type=pl.DeviceIdType.MESH,
        )

    started = []
    gain_copies = []

    def send_gain(stage):
        copy = remote(
            gain_val.at[stage],
            gain_in.at[stage],
            gain_send.at[stage],
            gain_recv.at[stage],
            partner(plans[0][stage][0]),
        )
        copy.start()
        gain_copies.append(copy)

    gain_local = jnp.sum(gain_ref[0, 0].astype(F32), axis=0, keepdims=True)
    gain_val[0] = gain_local.astype(BF16).astype(F32)
    send_gain(0)
    copies = []
    for p in range(PARTS):
        low, high = p * part_rows, (p + 1) * part_rows
        for half in range(2):
            for at, count, kind, col in blocks:
                start, stop = max(at, low), min(at + count, high)
                if start >= stop:
                    continue

                def fill(r, half=half, at=at, start=start, kind=kind, col=col):
                    if kind == "key":
                        first = pl.multiple_of(half * count_key + start - at + r, 16)
                        rows, cols = pl.ds(first, 64), slice(col, col + LANES)
                        source = key_ref
                    else:
                        first = pl.multiple_of(start - at + r, 16)
                        left = half * count_router + col
                        rows, cols = pl.ds(first, 64), slice(left, left + LANES)
                        source = router_ref
                    one = source[0, 0, 0, rows, cols].astype(F32)
                    two = source[0, 0, 1, rows, cols].astype(F32)
                    into = pl.ds(pl.multiple_of(start + r, 16), 64)
                    local[half, into, :] = (one + two).astype(BF16)

                count_key = key_ref.shape[3] // 2
                count_router = router_ref.shape[4] // 2
                rows_loop(stop - start, 64, fill)
        count = part_rows // 2
        sent = pl.multiple_of(low + (1 - bit[0]) * count, 16)
        copy = remote(
            local.at[:, pl.ds(sent, count), :],
            recv_bufs[p][0],
            send_sem.at[p, 0],
            recv_sem.at[p, 0],
            partner(0),
        )
        copy.start()
        copies.append(copy)
        started.append(copy)

    base = [pl.multiple_of(p * part_rows + bit[0] * (part_rows // 2), 16) for p in range(PARTS)]
    rows_now = [part_rows // 2] * PARTS
    split = [False] * PARTS

    def add(p, stage, half, h, offset, r, step):
        previous = local if stage == 0 else acc
        mine = previous[half, pl.ds(pl.multiple_of(base[p] + offset + r, 16), step), :]
        theirs = recv_bufs[p][stage][h, pl.ds(pl.multiple_of(offset + r, 16), step), :]
        return mine.astype(F32) + theirs.astype(F32)

    for stage in range(1, stages):
        gain_copies[stage - 1].wait_recv()
        gain_val[stage] = gain_val[stage - 1] + gain_in[stage - 1]
        send_gain(stage)
        fresh = []
        for p in range(PARTS):
            axis, shape = plans[p][stage]
            copies[p].wait_recv()
            halves = [(narrow, 0)] if split[p] else [(0, 0), (1, 1)]
            send_buf = send_bufs[p][stage - 1]
            step = 48
            if axis == "x":
                send_sets, keep_sets = [(1 - narrow, 1 - narrow, 0)], [(narrow, narrow)]
                send_offset = keep_offset = 0
            elif axis < HALVED_BITS:
                send_sets = [(half, h, h) for half, h in halves]
                keep_sets = halves
                send_offset = (1 - bit[axis]) * shape[1]
                keep_offset = bit[axis] * shape[1]
            else:
                send_sets, keep_sets = [(narrow, 0, 0)], []
                send_offset = keep_offset = 0

            def out(r, p=p):
                for half, h, slot in send_sets:
                    value = add(p, stage - 1, half, h, send_offset, r, step)
                    send_buf[slot, pl.ds(r, step), :] = value.astype(BF16)
                    if not keep_sets:
                        rows = pl.ds(pl.multiple_of(base[p] + r, 16), step)
                        acc[half, rows, :] = value.astype(BF16).astype(F32)

            rows_loop(shape[1], step, out)
            copy = remote(
                send_buf,
                recv_bufs[p][stage],
                send_sem.at[p, stage],
                recv_sem.at[p, stage],
                partner(axis),
            )
            copy.start()
            fresh.append(copy)
            started.append(copy)

            def keep(r, p=p):
                for half, h in keep_sets:
                    value = add(p, stage - 1, half, h, keep_offset, r, step)
                    rows = pl.ds(pl.multiple_of(base[p] + keep_offset + r, 16), step)
                    acc[half, rows, :] = value

            if keep_sets:
                rows_loop(shape[1], step, keep)
            if axis == "x":
                split[p] = True
            base[p] = pl.multiple_of(base[p] + keep_offset, 16)
            rows_now[p] = shape[1]
        copies = fresh

    gather_axes = [
        [3] + [a for a in reversed(part_orders()[p]) if a != "x"] + [0] for p in range(PARTS)
    ]
    gathers = []

    def gather(p, stage):
        rows = pl.ds(base[p], rows_now[p])
        axis = gather_axes[p][stage]
        copy = remote(
            full.at[rows, :],
            full.at[rows, :],
            gather_send.at[p, stage],
            gather_recv.at[p, stage],
            partner(axis),
        )
        copy.start()
        started.append(copy)
        base[p] = pl.multiple_of(base[p] - bit[axis] * rows_now[p], 16)
        rows_now[p] = 2 * rows_now[p]
        return copy

    squares = jnp.zeros((8, LANES), F32)
    for p in range(PARTS):
        copies[p].wait_recv()
        count = rows_now[p]
        value = add(p, stages - 1, narrow, 0, 0, 0, count)
        full[pl.ds(base[p], count), :] = value.astype(BF16)
        gathers.append(gather(p, 0))
        squares = squares + jnp.sum((value * value).reshape(count // 8, 8, LANES), axis=0)

    def send_square(source, slot, to):
        copy = remote(
            square_val.at[source],
            square_in.at[slot],
            square_send.at[slot],
            square_recv.at[slot],
            to,
        )
        copy.start()
        started.append(copy)
        return copy

    square_val[0] = squares
    square_copies = [
        send_square(0, 0, partner("x")),
        send_square(0, 1, partner(3)),
        send_square(0, 2, diagonal),
    ]
    gain_copies[stages - 1].wait_recv()
    gain_sum = gain_val[stages - 1] + gain_in[stages - 1]
    gain_val[stages] = gain_sum
    left = pl.multiple_of(narrow * gain_out.shape[1], 128)
    gain_out[...] = gain_val[stages, :, pl.ds(left, gain_out.shape[1])]
    for copy in square_copies:
        copy.wait_recv()
    square_val[1] = (square_val[0] + square_in[0]) + (square_in[1] + square_in[2])
    for stage in range(1, 4):
        square_copy = send_square(stage, stage + 2, partner((2, 1, 0)[stage - 1]))
        for p in range(PARTS):
            gathers[p].wait_recv()
            gathers[p] = gather(p, stage)
        square_copy.wait_recv()
        square_val[stage + 1] = square_val[stage] + square_in[stage + 2]
    total = jnp.sum(square_val[4]) + jnp.sum(gain_sum * gain_sum)
    total = jnp.full(factor_out.shape, total, F32)
    factor_out[...] = clip_limit / jnp.maximum(jnp.sqrt(total), clip_limit)
    for copy in gathers:
        copy.wait_recv()
    for at, count, kind, col in blocks:
        target = key_out if kind == "key" else router_out

        def place(r, at=at, col=col, target=target):
            rows = pl.ds(pl.multiple_of(at + r, 16), 64)
            target[pl.ds(r, 64), col : col + LANES] = full[rows, :]

        rows_loop(count, 64, place)
    for copy in started + gain_copies:
        copy.wait_send()


def reduce_grads(wide_size, key_grads, router_grads, gain_grads):
    key_shape, router_shape = key_grads.shape[3:], router_grads.shape[3:]
    gain_size = gain_grads.shape[3]
    blocks, total_rows = layout(key_shape, router_shape)
    wide_bits = wide_size.bit_length() - 1
    plans = stage_shapes(total_rows // PARTS, wide_bits)
    stages = len(plans[0])
    count = math.prod(key_shape) + math.prod(router_shape) + gain_size
    vmem = pl.BlockSpec(memory_space=pltpu.VMEM)
    return pl.pallas_call(
        functools.partial(
            reduce_kernel, plans, blocks, total_rows, 0.5 * math.sqrt(count)
        ),
        out_shape=(
            jax.ShapeDtypeStruct((key_shape[0] // 2, key_shape[1]), BF16),
            jax.ShapeDtypeStruct((router_shape[0], router_shape[1] // 2), BF16),
            jax.ShapeDtypeStruct((1, gain_size // 2), F32),
            jax.ShapeDtypeStruct((1, 128), F32),
        ),
        in_specs=[vmem] * 3,
        out_specs=(vmem,) * 4,
        scratch_shapes=[
            pltpu.VMEM((2, total_rows, LANES), BF16),
            pltpu.VMEM((2, total_rows, LANES), F32),
            pltpu.VMEM((total_rows, LANES), BF16),
            pltpu.VMEM((stages + 1, 1, gain_size), F32),
            pltpu.VMEM((stages, 1, gain_size), F32),
            pltpu.VMEM((5, 8, LANES), F32),
            pltpu.VMEM((6, 8, LANES), F32),
            [[pltpu.VMEM(shape, BF16) for _, shape in plan[1:]] for plan in plans],
            [[pltpu.VMEM(shape, BF16) for _, shape in plan] for plan in plans],
            pltpu.SemaphoreType.DMA((PARTS, stages)),
            pltpu.SemaphoreType.DMA((PARTS, stages)),
            pltpu.SemaphoreType.DMA((PARTS, 4)),
            pltpu.SemaphoreType.DMA((PARTS, 4)),
            pltpu.SemaphoreType.DMA((stages,)),
            pltpu.SemaphoreType.DMA((stages,)),
            pltpu.SemaphoreType.DMA((6,)),
            pltpu.SemaphoreType.DMA((6,)),
        ],
        compiler_params=pltpu.CompilerParams(
            collective_id=0, has_side_effects=True, vmem_limit_bytes=40 * 2**20
        ),
    )(key_grads, router_grads, gain_grads)


def on_device(
    wide_size,
    key_grads,
    router_grads,
    gain_grads,
    key_master,
    key_first,
    key_second,
    router_master,
    router_first,
    router_second,
    gain_master,
    gain_first,
    gain_second,
):
    key_sum, router_sum, gain_sum, factor = reduce_grads(
        wide_size, key_grads, router_grads, gain_grads
    )
    key_sum, router_sum = key_sum.astype(F32), router_sum.astype(F32)
    gain_sum, factor = gain_sum[0], factor[0, 0]
    key_new, key_first_new, key_second_new = adamw(
        key_master, key_first, key_second, key_sum, factor, 0.1
    )
    router_new, router_first_new, router_second_new = adamw(
        router_master, router_first, router_second, router_sum, factor, 0.1
    )
    gain_new, gain_first_new, gain_second_new = adamw(
        gain_master, gain_first, gain_second, gain_sum, factor, 0.0
    )
    key_weight, router_weight, gain_weight = (
        lax.all_gather(key_new.astype(BF16), "narrow", axis=0, tiled=True),
        lax.all_gather(router_new.astype(BF16), "narrow", axis=1, tiled=True),
        lax.all_gather(gain_new.astype(BF16), "narrow", axis=0, tiled=True),
    )
    return (
        key_new,
        key_first_new,
        key_second_new,
        router_new,
        router_first_new,
        router_second_new,
        gain_new,
        gain_first_new,
        gain_second_new,
        key_weight,
        router_weight,
        gain_weight,
    )


def solution(mesh):
    state = (P("narrow", None),) * 3 + (P(None, "narrow"),) * 3 + (P("narrow"),) * 3
    grads = (
        P("wide", "narrow", None, None, None),
        P("wide", "narrow", None, None, None),
        P("wide", "narrow", None, None),
    )
    return jax.shard_map(
        functools.partial(on_device, mesh.shape["wide"]),
        mesh=mesh,
        in_specs=grads + state,
        out_specs=state + (P(), P(), P()),
        check_vma=False,
    )
```

```python
import functools
import math

import jax
import jax.numpy as jnp
from jax import lax
from jax.experimental import pallas as pl
from jax.experimental.pallas import tpu as pltpu
from jax.sharding import PartitionSpec as P

beta_one = 0.9
beta_two = 0.95
step_rate = 0.01
epsilon = 1e-08
bias_one = 1.0 - 0.9**10
bias_two = 1.0 - 0.95**10

LANES = 256
PARTS = 3
HALVED_BITS = 4
KEY_PIECE = 64
F32, BF16 = jnp.float32, jnp.bfloat16


def adamw(master, first_moment, second, gradient, factor, decay_rate):
    scaled = factor * gradient
    first_new = beta_one * first_moment + (1.0 - beta_one) * scaled
    second_new = beta_two * second + (1.0 - beta_two) * scaled * scaled
    root = jnp.sqrt(second_new * (1.0 / bias_two)) + epsilon
    update = first_new * (1.0 / bias_one) / root
    if decay_rate:
        update = update + decay_rate * master
    return (master - step_rate * update, first_new, second_new)


def rows_loop(count, step, body):
    def one(i, carry):
        body(pl.multiple_of(i * step, 16))
        return carry

    lax.fori_loop(0, count // step, one, 0)


def layout(key_shape, router_shape):
    half_rows, half_cols = key_shape[0] // 2, router_shape[1] // 2
    blocks, at = [], 0
    for col in range(0, key_shape[1], LANES):
        blocks.append((at, half_rows, "key", col))
        at += half_rows
    for col in range(0, half_cols, LANES):
        blocks.append((at, router_shape[0], "router", col))
        at += router_shape[0]
    return blocks, at


def part_orders():
    return (("x", 1, 2), (1, 2, "x"), (2, "x", 1))


def stage_shapes(part_rows, wide_bits):
    plans = []
    for order in part_orders():
        halves, count, plan = 2, part_rows, []
        for axis in (0,) + order + (3,):
            if axis == "x":
                halves = 1
            else:
                count //= 2
            plan.append((axis, (halves, count, LANES)))
        for axis in range(HALVED_BITS, wide_bits):
            plan.append((axis, (halves, count, LANES)))
        plans.append(plan)
    return plans


def reduce_kernel(
    plans,
    blocks,
    total_rows,
    clip_limit,
    key_ref,
    router_ref,
    gain_ref,
    key_state,
    router_state,
    gain_state,
    key_out,
    router_out,
    gain_out,
    factor_out,
    key_other,
    router_other,
    gain_other,
    grads,
    gain_grads,
    local,
    acc,
    full,
    gain_val,
    gain_in,
    square_val,
    square_in,
    send_bufs,
    recv_bufs,
    send_sem,
    recv_sem,
    gather_send,
    gather_recv,
    gain_send,
    gain_recv,
    square_send,
    square_recv,
    key_mine,
    router_mine,
    gain_mine,
    key_weight,
    router_weight,
    key_far,
    router_far,
    gain_new,
    gain_far,
    load_sem,
    mine_sem,
    weight_send,
    weight_recv,
    gain_far_sem,
    out_sem,
):
    wide, narrow = lax.axis_index("wide"), lax.axis_index("narrow")
    stages = len(plans[0])
    part_rows = total_rows // PARTS
    wide_bits = stages - 1
    bit = [(wide // 2**k) % 2 for k in range(wide_bits)]

    def partner(axis):
        if axis == "x":
            return (wide, 1 - narrow)
        return (wide + (1 - 2 * bit[axis]) * 2**axis, narrow)

    half_rows, half_cols = key_ref.shape[3] // 2, router_ref.shape[4] // 2
    gain_load = pltpu.make_async_copy(gain_ref.at[0, 0], gain_grads, load_sem.at[0])
    gain_load.start()
    loads = []
    for p in range(PARTS):
        part_loads = []
        for half in range(2):
            for at, count, kind, col in blocks:
                start, stop = max(at, p * part_rows), min(at + count, (p + 1) * part_rows)
                if start >= stop:
                    continue
                first = start - at + (half * half_rows if kind == "key" else 0)
                left = col + (half * half_cols if kind == "router" else 0)
                source = key_ref if kind == "key" else router_ref
                copy = pltpu.make_async_copy(
                    source.at[0, 0, :, pl.ds(first, stop - start), pl.ds(left, LANES)],
                    grads.at[:, half, pl.ds(start, stop - start), :],
                    load_sem.at[1 + len(part_loads) + sum(map(len, loads))],
                )
                copy.start()
                part_loads.append(copy)
        loads.append(part_loads)

    quarter = 2 * bit[0] + bit[1]
    key_rows, router_rows = half_rows // 4, router_ref.shape[3] // 4
    mine_loads = []
    for i, (state, mine, count) in enumerate(
        [(r, key_mine, key_rows) for r in key_state]
        + [(r, router_mine, router_rows) for r in router_state]
        + [(r, gain_mine, 1) for r in gain_state]
    ):
        rows = pl.ds(pl.multiple_of(quarter * count, 16), count) if count > 1 else pl.ds(0, 1)
        copy = pltpu.make_async_copy(state.at[rows, :], mine.at[i % 3], mine_sem.at[i])
        copy.start()
        mine_loads.append(copy)

    diagonal = (partner(3)[0], 1 - narrow)
    friends = [partner(a) for a in ["x"] + list(range(wide_bits))] + [diagonal]
    barrier = pltpu.get_barrier_semaphore()
    for friend in friends:
        pl.semaphore_signal(barrier, inc=1, device_id=friend, device_id_type=pl.DeviceIdType.MESH)
    pl.semaphore_wait(barrier, len(friends))

    def remote(src, dst, send, recv, to):
        return pltpu.make_async_remote_copy(
            src_ref=src,
            dst_ref=dst,
            send_sem=send,
            recv_sem=recv,
            device_id=to,
            device_id_type=pl.DeviceIdType.MESH,
        )

    started = []
    gain_copies = []

    def send_gain(stage):
        copy = remote(
            gain_val.at[stage],
            gain_in.at[stage],
            gain_send.at[stage],
            gain_recv.at[stage],
            partner(plans[0][stage][0]),
        )
        copy.start()
        gain_copies.append(copy)

    gain_load.wait()
    gain_local = jnp.sum(gain_grads[...].astype(F32), axis=0, keepdims=True)
    gain_val[0] = gain_local.astype(BF16).astype(F32)
    send_gain(0)
    copies = []
    for p in range(PARTS):
        for load in loads[p]:
            load.wait()
        count = part_rows // 2
        sent = pl.multiple_of(p * part_rows + (1 - bit[0]) * count, 16)
        kept = pl.multiple_of(p * part_rows + bit[0] * count, 16)

        def fill(r, first):
            rows = pl.ds(pl.multiple_of(first + r, 16), 48)
            for half in range(2):
                one, two = grads[0, half, rows, :], grads[1, half, rows, :]
                local[half, rows, :] = (one.astype(F32) + two.astype(F32)).astype(BF16)

        rows_loop(count, 48, functools.partial(fill, first=sent))
        copy = remote(
            local.at[:, pl.ds(sent, count), :],
            recv_bufs[p][0],
            send_sem.at[p, 0],
            recv_sem.at[p, 0],
            partner(0),
        )
        copy.start()
        copies.append(copy)
        started.append(copy)
        rows_loop(count, 48, functools.partial(fill, first=kept))

    base = [pl.multiple_of(p * part_rows + bit[0] * (part_rows // 2), 16) for p in range(PARTS)]
    rows_now = [part_rows // 2] * PARTS
    split = [False] * PARTS

    def add(p, stage, half, h, offset, r, step):
        previous = local if stage == 0 else acc
        mine = previous[half, pl.ds(pl.multiple_of(base[p] + offset + r, 16), step), :]
        theirs = recv_bufs[p][stage][h, pl.ds(pl.multiple_of(offset + r, 16), step), :]
        return mine.astype(F32) + theirs.astype(F32)

    for stage in range(1, stages):
        gain_copies[stage - 1].wait_recv()
        gain_val[stage] = gain_val[stage - 1] + gain_in[stage - 1]
        send_gain(stage)
        fresh = []
        for p in range(PARTS):
            axis, shape = plans[p][stage]
            copies[p].wait_recv()
            halves = [(narrow, 0)] if split[p] else [(0, 0), (1, 1)]
            send_buf = send_bufs[p][stage - 1]
            step = 48
            if axis == "x":
                send_sets, keep_sets = [(1 - narrow, 1 - narrow, 0)], [(narrow, narrow)]
                send_offset = keep_offset = 0
            elif axis < HALVED_BITS:
                send_sets = [(half, h, h) for half, h in halves]
                keep_sets = halves
                send_offset = (1 - bit[axis]) * shape[1]
                keep_offset = bit[axis] * shape[1]
            else:
                send_sets, keep_sets = [(narrow, 0, 0)], []
                send_offset = keep_offset = 0

            def out(r, p=p):
                for half, h, slot in send_sets:
                    value = add(p, stage - 1, half, h, send_offset, r, step)
                    send_buf[slot, pl.ds(r, step), :] = value.astype(BF16)
                    if not keep_sets:
                        rows = pl.ds(pl.multiple_of(base[p] + r, 16), step)
                        acc[half, rows, :] = value.astype(BF16).astype(F32)

            rows_loop(shape[1], step, out)
            copy = remote(
                send_buf,
                recv_bufs[p][stage],
                send_sem.at[p, stage],
                recv_sem.at[p, stage],
                partner(axis),
            )
            copy.start()
            fresh.append(copy)
            started.append(copy)

            def keep(r, p=p):
                for half, h in keep_sets:
                    value = add(p, stage - 1, half, h, keep_offset, r, step)
                    rows = pl.ds(pl.multiple_of(base[p] + keep_offset + r, 16), step)
                    acc[half, rows, :] = value

            if keep_sets:
                rows_loop(shape[1], step, keep)
            if axis == "x":
                split[p] = True
            base[p] = pl.multiple_of(base[p] + keep_offset, 16)
            rows_now[p] = shape[1]
        copies = fresh

    gather_axes = [
        [3] + [a for a in reversed(part_orders()[p]) if a != "x"] + [0] for p in range(PARTS)
    ]
    gathers = []

    def gather(p, stage):
        rows = pl.ds(base[p], rows_now[p])
        axis = gather_axes[p][stage]
        copy = remote(
            full.at[rows, :],
            full.at[rows, :],
            gather_send.at[p, stage],
            gather_recv.at[p, stage],
            partner(axis),
        )
        copy.start()
        started.append(copy)
        base[p] = pl.multiple_of(base[p] - bit[axis] * rows_now[p], 16)
        rows_now[p] = 2 * rows_now[p]
        return copy

    squares = jnp.zeros((8, LANES), F32)
    for p in range(PARTS):
        copies[p].wait_recv()
        count = rows_now[p]
        value = add(p, stages - 1, narrow, 0, 0, 0, count)
        full[pl.ds(base[p], count), :] = value.astype(BF16)
        gathers.append(gather(p, 0))
        squares = squares + jnp.sum((value * value).reshape(count // 8, 8, LANES), axis=0)

    def send_square(source, slot, to):
        copy = remote(
            square_val.at[source],
            square_in.at[slot],
            square_send.at[slot],
            square_recv.at[slot],
            to,
        )
        copy.start()
        started.append(copy)
        return copy

    square_val[0] = squares
    square_copies = [
        send_square(0, 0, partner("x")),
        send_square(0, 1, partner(3)),
        send_square(0, 2, diagonal),
    ]
    gain_copies[stages - 1].wait_recv()
    gain_sum = gain_val[stages - 1] + gain_in[stages - 1]
    gain_val[stages] = gain_sum
    left = pl.multiple_of(narrow * gain_out.shape[1], 128)
    gain_out[...] = gain_val[stages, :, pl.ds(left, gain_out.shape[1])]
    for copy in square_copies:
        copy.wait_recv()
    square_val[1] = (square_val[0] + square_in[0]) + (square_in[1] + square_in[2])
    for stage in range(1, 4):
        square_copy = send_square(stage, stage + 2, partner((2, 1, 0)[stage - 1]))
        for p in range(PARTS):
            gathers[p].wait_recv()
            gathers[p] = gather(p, stage)
        square_copy.wait_recv()
        square_val[stage + 1] = square_val[stage] + square_in[stage + 2]
    total = jnp.sum(square_val[4]) + jnp.sum(gain_sum * gain_sum)
    total = jnp.full(factor_out.shape, total, F32)
    factor_out[...] = clip_limit / jnp.maximum(jnp.sqrt(total), clip_limit)
    for copy in gathers:
        copy.wait_recv()
    for copy in mine_loads:
        copy.wait()

    factor = factor_out[0:1, 0:1]
    gain_new[...] = adamw(
        gain_mine[0], gain_mine[1], gain_mine[2], gain_out[...], factor, 0.0
    )[0]
    gain_copy = remote(gain_new, gain_far, gain_far_sem.at[0], gain_far_sem.at[1], partner("x"))
    gain_copy.start()
    pieces = [("key", i * KEY_PIECE, KEY_PIECE) for i in range(key_rows // KEY_PIECE)]
    pieces.append(("router", 0, router_rows))

    def far(kind, q, first, count):
        buffer, size = (key_far, key_rows) if kind == "key" else (router_far, router_rows)
        return buffer.at[pl.ds(pl.multiple_of(q * size + first, 16), count), :]

    def forward(i, hop, q, axis):
        block = far(pieces[i][0], q, *pieces[i][1:])
        copy = remote(block, block, weight_send.at[hop, i], weight_recv.at[hop, i], partner(axis))
        copy.start()
        started.append(copy)
        return copy

    across = []
    for i, (kind, first, count) in enumerate(pieces):
        if kind == "key":
            mine, weight, size, height = key_mine, key_weight, key_rows, half_rows
        else:
            mine, weight, size, height = router_mine, router_weight, router_rows, 4 * router_rows
        for at, _, block_kind, col in blocks:
            if block_kind != kind:
                continue

            def step(r, at=at, col=col):
                r = pl.multiple_of(first + r, 16)
                rows, cols = pl.ds(r, 16), slice(col, col + LANES)
                gradient = full[pl.ds(pl.multiple_of(at + quarter * size + r, 16), 16), :]
                new = adamw(
                    mine[0, rows, cols],
                    mine[1, rows, cols],
                    mine[2, rows, cols],
                    gradient.astype(F32),
                    factor,
                    0.1,
                )[0]
                weight[rows, cols] = new.astype(BF16)

            rows_loop(count, 16, step)
        copy = remote(
            weight.at[pl.ds(first, count), :],
            far(kind, quarter, first, count),
            weight_send.at[0, i],
            weight_recv.at[0, i],
            partner("x"),
        )
        copy.start()
        started.append(copy)
        across.append(copy)

    out_copies = []

    def leave(source, target):
        copy = pltpu.make_async_copy(source, target, out_sem.at[len(out_copies)])
        copy.start()
        out_copies.append(copy)

    for at, count, kind, col in blocks:
        target = key_out if kind == "key" else router_out
        leave(full.at[pl.ds(at, count), :], target.at[:, pl.ds(col, LANES)])

    beside, own, other = [], [], []
    for i, copy in enumerate(across):
        copy.wait_recv()
        beside.append(forward(i, 1, quarter, 1))
        own.append(forward(i, 2, quarter, 0))
    neighbour = 2 * bit[0] + 1 - bit[1]
    for i, copy in enumerate(beside):
        copy.wait_recv()
        other.append(forward(i, 3, neighbour, 0))
    gain_copy.wait_recv()
    gain_other[...] = gain_far[...]
    for copy in own + other:
        copy.wait_recv()
    leave(key_far, key_other)
    leave(router_far, router_other)
    for copy in started + gain_copies + [gain_copy]:
        copy.wait_send()
    for copy in out_copies:
        copy.wait()


def update_kernel(
    key_grad,
    router_grad,
    gain_grad,
    factor_ref,
    key_other,
    router_other,
    gain_other,
    key_state,
    router_state,
    gain_state,
    key_new,
    router_new,
    gain_new,
    key_weight,
    router_weight,
    gain_weight,
):
    narrow = lax.axis_index("narrow")
    factor = factor_ref[0:1, 0:1]

    def update(state, grad, decay_rate, new):
        values = adamw(
            state[0][...], state[1][...], state[2][...], grad[...].astype(F32), factor, decay_rate
        )
        for ref, value in zip(new, values):
            ref[...] = value
        return values[0].astype(BF16)

    key_weight[narrow] = update(key_state, key_grad, 0.1, key_new)
    key_weight[1 - narrow] = key_other[...]

    def columns(n, size):
        return pl.ds(pl.multiple_of(n * size, 128), size)

    size = router_other.shape[1]
    router_weight[:, columns(narrow, size)] = update(router_state, router_grad, 0.1, router_new)
    router_weight[:, columns(1 - narrow, size)] = router_other[...]
    size = gain_other.shape[1]
    gain_weight[:, columns(narrow, size)] = update(gain_state, gain_grad, 0.0, gain_new)
    gain_weight[:, columns(1 - narrow, size)] = gain_other[...].astype(BF16)


def update_all(sums, key_state, router_state, gain_state):
    steps = 4
    key_sum, router_sum, gain_sum, factor, key_other, router_other, gain_other = sums
    (rows, width), (experts, cols), (_, gain) = key_sum.shape, router_sum.shape, gain_sum.shape
    key_spec = pl.BlockSpec((rows // steps, width), lambda i: (i, 0))
    router_spec = pl.BlockSpec((experts // steps, cols), lambda i: (i, 0))
    gain_spec = pl.BlockSpec((1, gain), lambda i: (0, 0))
    shape = jax.ShapeDtypeStruct
    return pl.pallas_call(
        update_kernel,
        grid=(steps,),
        out_shape=(
            [shape((rows, width), F32)] * 3,
            [shape((experts, cols), F32)] * 3,
            [shape((1, gain), F32)] * 3,
            shape((2, rows, width), BF16),
            shape((experts, 2 * cols), BF16),
            shape((1, 2 * gain), BF16),
        ),
        in_specs=[
            key_spec,
            router_spec,
            gain_spec,
            pl.BlockSpec((1, 128), lambda i: (0, 0)),
            key_spec,
            router_spec,
            gain_spec,
            [key_spec] * 3,
            [router_spec] * 3,
            [gain_spec] * 3,
        ],
        out_specs=(
            [key_spec] * 3,
            [router_spec] * 3,
            [gain_spec] * 3,
            pl.BlockSpec((2, rows // steps, width), lambda i: (0, i, 0)),
            pl.BlockSpec((experts // steps, 2 * cols), lambda i: (i, 0)),
            pl.BlockSpec((1, 2 * gain), lambda i: (0, 0)),
        ),
        compiler_params=pltpu.CompilerParams(vmem_limit_bytes=40 * 2**20),
    )(
        key_sum,
        router_sum,
        gain_sum,
        factor,
        key_other,
        router_other,
        gain_other,
        key_state,
        router_state,
        gain_state,
    )


def reduce_grads(
    wide_size, key_grads, router_grads, gain_grads, key_state, router_state, gain_state
):
    key_shape, router_shape = key_grads.shape[3:], router_grads.shape[3:]
    gain_size = gain_grads.shape[3]
    blocks, total_rows = layout(key_shape, router_shape)
    wide_bits = wide_size.bit_length() - 1
    plans = stage_shapes(total_rows // PARTS, wide_bits)
    stages = len(plans[0])
    count = math.prod(key_shape) + math.prod(router_shape) + gain_size
    vmem = pl.BlockSpec(memory_space=pltpu.VMEM)
    hbm = pl.BlockSpec(memory_space=pl.ANY)
    half_rows, width = key_shape[0] // 2, key_shape[1]
    experts, half_cols = router_shape[0], router_shape[1] // 2
    pieces = half_rows // 4 // KEY_PIECE + 1
    return pl.pallas_call(
        functools.partial(
            reduce_kernel, plans, blocks, total_rows, 0.5 * math.sqrt(count)
        ),
        out_shape=(
            jax.ShapeDtypeStruct((key_shape[0] // 2, key_shape[1]), BF16),
            jax.ShapeDtypeStruct((router_shape[0], router_shape[1] // 2), BF16),
            jax.ShapeDtypeStruct((1, gain_size // 2), F32),
            jax.ShapeDtypeStruct((1, 128), F32),
            jax.ShapeDtypeStruct((half_rows, width), BF16),
            jax.ShapeDtypeStruct((experts, half_cols), BF16),
            jax.ShapeDtypeStruct((1, gain_size // 2), F32),
        ),
        in_specs=[hbm] * 3 + [[hbm] * 3] * 3,
        out_specs=(hbm, hbm, vmem, vmem, hbm, hbm, vmem),
        scratch_shapes=[
            pltpu.VMEM((2, 2, total_rows, LANES), BF16),
            pltpu.VMEM((2, gain_size), BF16),
            pltpu.VMEM((2, total_rows, LANES), BF16),
            pltpu.VMEM((2, total_rows, LANES), F32),
            pltpu.VMEM((total_rows, LANES), BF16),
            pltpu.VMEM((stages + 1, 1, gain_size), F32),
            pltpu.VMEM((stages, 1, gain_size), F32),
            pltpu.VMEM((5, 8, LANES), F32),
            pltpu.VMEM((6, 8, LANES), F32),
            [[pltpu.VMEM(shape, BF16) for _, shape in plan[1:]] for plan in plans],
            [[pltpu.VMEM(shape, BF16) for _, shape in plan] for plan in plans],
            pltpu.SemaphoreType.DMA((PARTS, stages)),
            pltpu.SemaphoreType.DMA((PARTS, stages)),
            pltpu.SemaphoreType.DMA((PARTS, 4)),
            pltpu.SemaphoreType.DMA((PARTS, 4)),
            pltpu.SemaphoreType.DMA((stages,)),
            pltpu.SemaphoreType.DMA((stages,)),
            pltpu.SemaphoreType.DMA((6,)),
            pltpu.SemaphoreType.DMA((6,)),
            pltpu.VMEM((3, half_rows // 4, width), F32),
            pltpu.VMEM((3, experts // 4, half_cols), F32),
            pltpu.VMEM((3, 1, gain_size // 2), F32),
            pltpu.VMEM((half_rows // 4, width), BF16),
            pltpu.VMEM((experts // 4, half_cols), BF16),
            pltpu.VMEM((half_rows, width), BF16),
            pltpu.VMEM((experts, half_cols), BF16),
            pltpu.VMEM((1, gain_size // 2), F32),
            pltpu.VMEM((1, gain_size // 2), F32),
            pltpu.SemaphoreType.DMA((2 * (len(blocks) + PARTS) + 1,)),
            pltpu.SemaphoreType.DMA((9,)),
            pltpu.SemaphoreType.DMA((4, pieces)),
            pltpu.SemaphoreType.DMA((4, pieces)),
            pltpu.SemaphoreType.DMA((2,)),
            pltpu.SemaphoreType.DMA((len(blocks) + 2,)),
        ],
        compiler_params=pltpu.CompilerParams(
            collective_id=0, has_side_effects=True, vmem_limit_bytes=56 * 2**20
        ),
    )(key_grads, router_grads, gain_grads, key_state, router_state, gain_state)


def on_device(
    wide_size,
    key_grads,
    router_grads,
    gain_grads,
    key_master,
    key_first,
    key_second,
    router_master,
    router_first,
    router_second,
    gain_master,
    gain_first,
    gain_second,
):
    key_state = [key_master, key_first, key_second]
    router_state = [router_master, router_first, router_second]
    gain_state = [x.reshape(1, -1) for x in (gain_master, gain_first, gain_second)]
    sums = reduce_grads(
        wide_size, key_grads, router_grads, gain_grads, key_state, router_state, gain_state
    )
    key_new, router_new, gain_new, key_weight, router_weight, gain_weight = update_all(
        sums, key_state, router_state, gain_state
    )
    return (
        *key_new,
        *router_new,
        *[x.reshape(-1) for x in gain_new],
        key_weight.reshape(-1, key_weight.shape[2]),
        router_weight,
        gain_weight.reshape(-1),
    )


def solution(mesh):
    state = (P("narrow", None),) * 3 + (P(None, "narrow"),) * 3 + (P("narrow"),) * 3
    grads = (
        P("wide", "narrow", None, None, None),
        P("wide", "narrow", None, None, None),
        P("wide", "narrow", None, None),
    )
    return jax.shard_map(
        functools.partial(on_device, mesh.shape["wide"]),
        mesh=mesh,
        in_specs=grads + state,
        out_specs=state + (P(), P(), P()),
        check_vma=False,
    )
```

```python
import functools
import math

import jax
import jax.numpy as jnp
from jax import lax
from jax.experimental import pallas as pl
from jax.experimental.pallas import tpu as pltpu
from jax.sharding import PartitionSpec as P

beta_one = 0.9
beta_two = 0.95
step_rate = 0.01
epsilon = 1e-08
bias_one = 1.0 - 0.9**10
bias_two = 1.0 - 0.95**10

LANES = 128
PARTS = 6
HALVED_BITS = 4
KEY_PIECE = 64
F32, BF16 = jnp.float32, jnp.bfloat16


def adamw(master, first_moment, second, gradient, factor, decay_rate):
    scaled = factor * gradient
    first_new = beta_one * first_moment + (1.0 - beta_one) * scaled
    second_new = beta_two * second + (1.0 - beta_two) * scaled * scaled
    root = jnp.sqrt(second_new * (1.0 / bias_two)) + epsilon
    update = first_new * (1.0 / bias_one) / root
    if decay_rate:
        update = update + decay_rate * master
    return (master - step_rate * update, first_new, second_new)


def rows_loop(count, step, body):
    def one(i, carry):
        body(pl.multiple_of(i * step, 16))
        return carry

    lax.fori_loop(0, count // step, one, 0)


def layout(key_shape, router_shape):
    half_rows, half_cols = key_shape[0] // 2, router_shape[1] // 2
    blocks, at = [], 0
    for col in range(0, key_shape[1], LANES):
        blocks.append((at, half_rows, "key", col))
        at += half_rows
    for col in range(0, half_cols, LANES):
        blocks.append((at, router_shape[0], "router", col))
        at += router_shape[0]
    return blocks, at


def part_orders():
    return (("x", 1, 2), (1, 2, "x"), (2, "x", 1)) * (PARTS // 3)


def stage_shapes(part_rows, wide_bits):
    plans = []
    for order in part_orders():
        halves, count, plan = 2, part_rows, []
        for axis in (0,) + order + (3,):
            if axis == "x":
                halves = 1
            else:
                count //= 2
            plan.append((axis, (halves, count, LANES)))
        for axis in range(HALVED_BITS, wide_bits):
            plan.append((axis, (halves, count, LANES)))
        plans.append(plan)
    return plans


def reduce_kernel(
    plans,
    blocks,
    total_rows,
    clip_limit,
    key_ref,
    router_ref,
    gain_ref,
    key_state,
    router_state,
    gain_state,
    key_out,
    router_out,
    gain_out,
    factor_out,
    key_other,
    router_other,
    gain_other,
    grads,
    gain_grads,
    local,
    acc,
    full,
    gain_val,
    gain_in,
    square_val,
    square_in,
    send_bufs,
    recv_bufs,
    send_sem,
    recv_sem,
    gather_send,
    gather_recv,
    gain_send,
    gain_recv,
    square_send,
    square_recv,
    key_mine,
    router_mine,
    gain_mine,
    key_weight,
    router_weight,
    key_far,
    router_far,
    gain_new,
    gain_far,
    load_sem,
    mine_sem,
    weight_send,
    weight_recv,
    gain_far_sem,
    out_sem,
):
    wide, narrow = lax.axis_index("wide"), lax.axis_index("narrow")
    stages = len(plans[0])
    part_rows = total_rows // PARTS
    wide_bits = stages - 1
    bit = [(wide // 2**k) % 2 for k in range(wide_bits)]

    def partner(axis):
        if axis == "x":
            return (wide, 1 - narrow)
        return (wide + (1 - 2 * bit[axis]) * 2**axis, narrow)

    diagonal = (partner(3)[0], 1 - narrow)
    friends = [partner(a) for a in ["x"] + list(range(wide_bits))] + [diagonal]
    barrier = pltpu.get_barrier_semaphore()
    for friend in friends:
        pl.semaphore_signal(barrier, inc=1, device_id=friend, device_id_type=pl.DeviceIdType.MESH)
    half_rows, half_cols = key_ref.shape[3] // 2, router_ref.shape[4] // 2
    gain_load = pltpu.make_async_copy(gain_ref.at[0, 0], gain_grads, load_sem.at[0])
    gain_load.start()
    loads = []
    for p in range(PARTS):
        part_loads = []
        for half in range(2):
            for at, count, kind, col in blocks:
                start, stop = max(at, p * part_rows), min(at + count, (p + 1) * part_rows)
                if start >= stop:
                    continue
                first = start - at + (half * half_rows if kind == "key" else 0)
                left = col + (half * half_cols if kind == "router" else 0)
                source = key_ref if kind == "key" else router_ref
                copy = pltpu.make_async_copy(
                    source.at[0, 0, :, pl.ds(first, stop - start), pl.ds(left, LANES)],
                    grads.at[:, half, pl.ds(start, stop - start), :],
                    load_sem.at[1 + len(part_loads) + sum(map(len, loads))],
                )
                copy.start()
                part_loads.append(copy)
        loads.append(part_loads)

    quarter = 2 * bit[0] + bit[1]
    key_rows, router_rows = half_rows // 4, router_ref.shape[3] // 4
    mine_loads = []
    for i, (state, mine, count) in enumerate(
        [(r, key_mine, key_rows) for r in key_state]
        + [(r, router_mine, router_rows) for r in router_state]
        + [(r, gain_mine, 1) for r in gain_state]
    ):
        rows = pl.ds(pl.multiple_of(quarter * count, 16), count) if count > 1 else pl.ds(0, 1)
        copy = pltpu.make_async_copy(state.at[rows, :], mine.at[i % 3], mine_sem.at[i])
        copy.start()
        mine_loads.append(copy)

    pl.semaphore_wait(barrier, len(friends))

    def remote(src, dst, send, recv, to):
        return pltpu.make_async_remote_copy(
            src_ref=src,
            dst_ref=dst,
            send_sem=send,
            recv_sem=recv,
            device_id=to,
            device_id_type=pl.DeviceIdType.MESH,
        )

    started = []
    gain_copies = []

    def send_gain(stage):
        copy = remote(
            gain_val.at[stage],
            gain_in.at[stage],
            gain_send.at[stage],
            gain_recv.at[stage],
            partner(plans[0][stage][0]),
        )
        copy.start()
        gain_copies.append(copy)

    gain_load.wait()
    gain_local = jnp.sum(gain_grads[...].astype(F32), axis=0, keepdims=True)
    gain_val[0] = gain_local.astype(BF16).astype(F32)
    send_gain(0)
    copies = []
    for p in range(PARTS):
        for load in loads[p]:
            load.wait()
        count = part_rows // 2
        sent = pl.multiple_of(p * part_rows + (1 - bit[0]) * count, 16)
        kept = pl.multiple_of(p * part_rows + bit[0] * count, 16)

        def fill(r, first):
            rows = pl.ds(pl.multiple_of(first + r, 16), 96)
            for half in range(2):
                local[half, rows, :] = grads[0, half, rows, :] + grads[1, half, rows, :]

        rows_loop(count, 96, functools.partial(fill, first=sent))
        copy = remote(
            local.at[:, pl.ds(sent, count), :],
            recv_bufs[p][0],
            send_sem.at[p, 0],
            recv_sem.at[p, 0],
            partner(0),
        )
        copy.start()
        copies.append(copy)
        started.append(copy)
        rows_loop(count, 96, functools.partial(fill, first=kept))

    base = [pl.multiple_of(p * part_rows + bit[0] * (part_rows // 2), 16) for p in range(PARTS)]
    rows_now = [part_rows // 2] * PARTS
    split = [False] * PARTS

    def add(p, stage, half, h, offset, r, step):
        previous = local if stage == 0 else acc
        mine = previous[half, pl.ds(pl.multiple_of(base[p] + offset + r, 16), step), :]
        theirs = recv_bufs[p][stage][h, pl.ds(pl.multiple_of(offset + r, 16), step), :]
        return mine.astype(F32) + theirs.astype(F32)

    for stage in range(1, stages):
        gain_copies[stage - 1].wait_recv()
        gain_val[stage] = gain_val[stage - 1] + gain_in[stage - 1]
        send_gain(stage)
        fresh = []
        for p in range(PARTS):
            axis, shape = plans[p][stage]
            copies[p].wait_recv()
            halves = [(narrow, 0)] if split[p] else [(0, 0), (1, 1)]
            send_buf = send_bufs[p][stage - 1]
            step = min(96, shape[1])
            if axis == "x":
                send_sets, keep_sets = [(1 - narrow, 1 - narrow, 0)], [(narrow, narrow)]
                send_offset = keep_offset = 0
            elif axis < HALVED_BITS:
                send_sets = [(half, h, h) for half, h in halves]
                keep_sets = halves
                send_offset = (1 - bit[axis]) * shape[1]
                keep_offset = bit[axis] * shape[1]
            else:
                send_sets, keep_sets = [(narrow, 0, 0)], []
                send_offset = keep_offset = 0

            def out(r, p=p):
                for half, h, slot in send_sets:
                    value = add(p, stage - 1, half, h, send_offset, r, step)
                    send_buf[slot, pl.ds(r, step), :] = value.astype(BF16)
                    if not keep_sets:
                        rows = pl.ds(pl.multiple_of(base[p] + r, 16), step)
                        acc[half, rows, :] = value.astype(BF16).astype(F32)

            rows_loop(shape[1], step, out)
            copy = remote(
                send_buf,
                recv_bufs[p][stage],
                send_sem.at[p, stage],
                recv_sem.at[p, stage],
                partner(axis),
            )
            copy.start()
            fresh.append(copy)
            started.append(copy)

            def keep(r, p=p):
                for half, h in keep_sets:
                    value = add(p, stage - 1, half, h, keep_offset, r, step)
                    rows = pl.ds(pl.multiple_of(base[p] + keep_offset + r, 16), step)
                    acc[half, rows, :] = value

            if keep_sets:
                rows_loop(shape[1], step, keep)
            if axis == "x":
                split[p] = True
            base[p] = pl.multiple_of(base[p] + keep_offset, 16)
            rows_now[p] = shape[1]
        copies = fresh

    gather_axes = [
        [3] + [a for a in reversed(part_orders()[p]) if a != "x"] + [0] for p in range(PARTS)
    ]
    gathers = []

    def gather(p, stage):
        rows = pl.ds(base[p], rows_now[p])
        axis = gather_axes[p][stage]
        copy = remote(
            full.at[rows, :],
            full.at[rows, :],
            gather_send.at[p, stage],
            gather_recv.at[p, stage],
            partner(axis),
        )
        copy.start()
        started.append(copy)
        base[p] = pl.multiple_of(base[p] - bit[axis] * rows_now[p], 16)
        rows_now[p] = 2 * rows_now[p]
        return copy

    squares = jnp.zeros((8, LANES), F32)
    for p in range(PARTS):
        copies[p].wait_recv()
        count = rows_now[p]
        value = add(p, stages - 1, narrow, 0, 0, 0, count)
        full[pl.ds(base[p], count), :] = value.astype(BF16)
        gathers.append(gather(p, 0))
        squares = squares + jnp.sum((value * value).reshape(count // 8, 8, LANES), axis=0)

    def send_square(source, slot, to):
        copy = remote(
            square_val.at[source],
            square_in.at[slot],
            square_send.at[slot],
            square_recv.at[slot],
            to,
        )
        copy.start()
        started.append(copy)
        return copy

    square_val[0] = squares
    square_copies = [
        send_square(0, 0, partner("x")),
        send_square(0, 1, partner(3)),
        send_square(0, 2, diagonal),
    ]
    gain_copies[stages - 1].wait_recv()
    gain_sum = gain_val[stages - 1] + gain_in[stages - 1]
    gain_val[stages] = gain_sum
    left = pl.multiple_of(narrow * gain_out.shape[1], 128)
    gain_out[...] = gain_val[stages, :, pl.ds(left, gain_out.shape[1])]
    for copy in square_copies:
        copy.wait_recv()
    square_val[1] = (square_val[0] + square_in[0]) + (square_in[1] + square_in[2])
    for stage in range(1, 4):
        square_copy = send_square(stage, stage + 2, partner((2, 1, 0)[stage - 1]))
        for p in range(PARTS):
            gathers[p].wait_recv()
            gathers[p] = gather(p, stage)
        square_copy.wait_recv()
        square_val[stage + 1] = square_val[stage] + square_in[stage + 2]
    total = jnp.sum(square_val[4]) + jnp.sum(gain_sum * gain_sum)
    total = jnp.full(factor_out.shape, total, F32)
    factor_out[...] = clip_limit / jnp.maximum(jnp.sqrt(total), clip_limit)
    for copy in gathers:
        copy.wait_recv()
    for copy in mine_loads:
        copy.wait()

    factor = factor_out[0:1, 0:1]
    gain_new[...] = adamw(
        gain_mine[0], gain_mine[1], gain_mine[2], gain_out[...], factor, 0.0
    )[0]
    gain_copy = remote(gain_new, gain_far, gain_far_sem.at[0], gain_far_sem.at[1], partner("x"))
    gain_copy.start()
    pieces = [("key", i * KEY_PIECE, KEY_PIECE) for i in range(key_rows // KEY_PIECE)]
    pieces.append(("router", 0, router_rows))

    def far(kind, q, first, count):
        buffer, size = (key_far, key_rows) if kind == "key" else (router_far, router_rows)
        return buffer.at[pl.ds(pl.multiple_of(q * size + first, 16), count), :]

    def forward(i, hop, q, axis):
        block = far(pieces[i][0], q, *pieces[i][1:])
        copy = remote(block, block, weight_send.at[hop, i], weight_recv.at[hop, i], partner(axis))
        copy.start()
        started.append(copy)
        return copy

    across = []
    for i, (kind, first, count) in enumerate(pieces):
        if kind == "key":
            mine, weight, size = key_mine, key_weight, key_rows
        else:
            mine, weight, size = router_mine, router_weight, router_rows
        for at, _, block_kind, col in blocks:
            if block_kind != kind:
                continue

            rows, cols = slice(first, first + count), slice(col, col + LANES)
            start = pl.multiple_of(at + quarter * size + first, 16)
            gradient = full[pl.ds(start, count), :].astype(F32)
            state = [mine[j, rows, cols] for j in range(3)]
            weight[rows, cols] = adamw(*state, gradient, factor, 0.1)[0].astype(BF16)
        copy = remote(
            weight.at[pl.ds(first, count), :],
            far(kind, quarter, first, count),
            weight_send.at[0, i],
            weight_recv.at[0, i],
            partner("x"),
        )
        copy.start()
        started.append(copy)
        across.append(copy)

    out_copies = []

    def leave(source, target):
        copy = pltpu.make_async_copy(source, target, out_sem.at[len(out_copies)])
        copy.start()
        out_copies.append(copy)

    for at, count, kind, col in blocks:
        target = key_out if kind == "key" else router_out
        leave(full.at[pl.ds(at, count), :], target.at[:, pl.ds(col, LANES)])

    beside, own, other = [], [], []
    for i, copy in enumerate(across):
        copy.wait_recv()
        beside.append(forward(i, 1, quarter, 1))
        own.append(forward(i, 2, quarter, 0))
    neighbour = 2 * bit[0] + 1 - bit[1]
    for i, copy in enumerate(beside):
        copy.wait_recv()
        other.append(forward(i, 3, neighbour, 0))
    gain_copy.wait_recv()
    gain_other[...] = gain_far[...]
    for copy in own + other:
        copy.wait_recv()
    leave(key_far, key_other)
    leave(router_far, router_other)
    for copy in started + gain_copies + [gain_copy]:
        copy.wait_send()
    for copy in out_copies:
        copy.wait()


def update_kernel(
    key_grad,
    router_grad,
    gain_grad,
    factor_ref,
    key_other,
    router_other,
    gain_other,
    key_state,
    router_state,
    gain_state,
    key_new,
    router_new,
    gain_new,
    key_weight,
    router_weight,
    gain_weight,
):
    narrow = lax.axis_index("narrow")
    factor = factor_ref[0:1, 0:1]

    def update(state, grad, decay_rate, new, rows):
        old = [ref[rows, :] for ref in state]
        values = adamw(*old, grad[rows, :].astype(F32), factor, decay_rate)
        for ref, value in zip(new, values):
            ref[rows, :] = value
        return values[0].astype(BF16)

    def key_step(r):
        rows = pl.ds(r, 32)
        key_weight[narrow, rows, :] = update(key_state, key_grad, 0.1, key_new, rows)
        key_weight[1 - narrow, rows, :] = key_other[rows, :]

    rows_loop(key_grad.shape[0], 32, key_step)

    def columns(n, size):
        return pl.ds(pl.multiple_of(n * size, 128), size)

    size = router_other.shape[1]
    router_weight[:, columns(narrow, size)] = update(
        router_state, router_grad, 0.1, router_new, slice(None)
    )
    router_weight[:, columns(1 - narrow, size)] = router_other[...]
    size = gain_other.shape[1]
    gain_weight[:, columns(narrow, size)] = update(
        gain_state, gain_grad, 0.0, gain_new, slice(None)
    )
    gain_weight[:, columns(1 - narrow, size)] = gain_other[...].astype(BF16)


def update_all(sums, key_state, router_state, gain_state):
    steps = 4
    key_sum, router_sum, gain_sum, factor, key_other, router_other, gain_other = sums
    (rows, width), (experts, cols), (_, gain) = key_sum.shape, router_sum.shape, gain_sum.shape
    key_spec = pl.BlockSpec((rows // steps, width), lambda i: (i, 0))
    router_spec = pl.BlockSpec((experts // steps, cols), lambda i: (i, 0))
    gain_spec = pl.BlockSpec((1, gain), lambda i: (0, 0))
    shape = jax.ShapeDtypeStruct
    return pl.pallas_call(
        update_kernel,
        grid=(steps,),
        out_shape=(
            [shape((rows, width), F32)] * 3,
            [shape((experts, cols), F32)] * 3,
            [shape((1, gain), F32)] * 3,
            shape((2, rows, width), BF16),
            shape((experts, 2 * cols), BF16),
            shape((1, 2 * gain), BF16),
        ),
        in_specs=[
            key_spec,
            router_spec,
            gain_spec,
            pl.BlockSpec((1, 128), lambda i: (0, 0)),
            key_spec,
            router_spec,
            gain_spec,
            [key_spec] * 3,
            [router_spec] * 3,
            [gain_spec] * 3,
        ],
        out_specs=(
            [key_spec] * 3,
            [router_spec] * 3,
            [gain_spec] * 3,
            pl.BlockSpec((2, rows // steps, width), lambda i: (0, i, 0)),
            pl.BlockSpec((experts // steps, 2 * cols), lambda i: (i, 0)),
            pl.BlockSpec((1, 2 * gain), lambda i: (0, 0)),
        ),
        compiler_params=pltpu.CompilerParams(vmem_limit_bytes=62 * 2**20),
    )(
        key_sum,
        router_sum,
        gain_sum,
        factor,
        key_other,
        router_other,
        gain_other,
        key_state,
        router_state,
        gain_state,
    )


def reduce_grads(
    wide_size, key_grads, router_grads, gain_grads, key_state, router_state, gain_state
):
    key_shape, router_shape = key_grads.shape[3:], router_grads.shape[3:]
    gain_size = gain_grads.shape[3]
    blocks, total_rows = layout(key_shape, router_shape)
    wide_bits = wide_size.bit_length() - 1
    plans = stage_shapes(total_rows // PARTS, wide_bits)
    stages = len(plans[0])
    count = math.prod(key_shape) + math.prod(router_shape) + gain_size
    vmem = pl.BlockSpec(memory_space=pltpu.VMEM)
    hbm = pl.BlockSpec(memory_space=pl.ANY)
    half_rows, width = key_shape[0] // 2, key_shape[1]
    experts, half_cols = router_shape[0], router_shape[1] // 2
    pieces = half_rows // 4 // KEY_PIECE + 1
    return pl.pallas_call(
        functools.partial(
            reduce_kernel, plans, blocks, total_rows, 0.5 * math.sqrt(count)
        ),
        out_shape=(
            jax.ShapeDtypeStruct((key_shape[0] // 2, key_shape[1]), BF16),
            jax.ShapeDtypeStruct((router_shape[0], router_shape[1] // 2), BF16),
            jax.ShapeDtypeStruct((1, gain_size // 2), F32),
            jax.ShapeDtypeStruct((1, 128), F32),
            jax.ShapeDtypeStruct((half_rows, width), BF16),
            jax.ShapeDtypeStruct((experts, half_cols), BF16),
            jax.ShapeDtypeStruct((1, gain_size // 2), F32),
        ),
        in_specs=[hbm] * 3 + [[hbm] * 3] * 3,
        out_specs=(hbm, hbm, vmem, vmem, hbm, hbm, vmem),
        scratch_shapes=[
            pltpu.VMEM((2, 2, total_rows, LANES), BF16),
            pltpu.VMEM((2, gain_size), BF16),
            pltpu.VMEM((2, total_rows, LANES), BF16),
            pltpu.VMEM((2, total_rows, LANES), F32),
            pltpu.VMEM((total_rows, LANES), BF16),
            pltpu.VMEM((stages + 1, 1, gain_size), F32),
            pltpu.VMEM((stages, 1, gain_size), F32),
            pltpu.VMEM((5, 8, LANES), F32),
            pltpu.VMEM((6, 8, LANES), F32),
            [[pltpu.VMEM(shape, BF16) for _, shape in plan[1:]] for plan in plans],
            [[pltpu.VMEM(shape, BF16) for _, shape in plan] for plan in plans],
            pltpu.SemaphoreType.DMA((PARTS, stages)),
            pltpu.SemaphoreType.DMA((PARTS, stages)),
            pltpu.SemaphoreType.DMA((PARTS, 4)),
            pltpu.SemaphoreType.DMA((PARTS, 4)),
            pltpu.SemaphoreType.DMA((stages,)),
            pltpu.SemaphoreType.DMA((stages,)),
            pltpu.SemaphoreType.DMA((6,)),
            pltpu.SemaphoreType.DMA((6,)),
            pltpu.VMEM((3, half_rows // 4, width), F32),
            pltpu.VMEM((3, experts // 4, half_cols), F32),
            pltpu.VMEM((3, 1, gain_size // 2), F32),
            pltpu.VMEM((half_rows // 4, width), BF16),
            pltpu.VMEM((experts // 4, half_cols), BF16),
            pltpu.VMEM((half_rows, width), BF16),
            pltpu.VMEM((experts, half_cols), BF16),
            pltpu.VMEM((1, gain_size // 2), F32),
            pltpu.VMEM((1, gain_size // 2), F32),
            pltpu.SemaphoreType.DMA((2 * (len(blocks) + PARTS) + 1,)),
            pltpu.SemaphoreType.DMA((9,)),
            pltpu.SemaphoreType.DMA((4, pieces)),
            pltpu.SemaphoreType.DMA((4, pieces)),
            pltpu.SemaphoreType.DMA((2,)),
            pltpu.SemaphoreType.DMA((len(blocks) + 2,)),
        ],
        compiler_params=pltpu.CompilerParams(
            collective_id=0, has_side_effects=True, vmem_limit_bytes=56 * 2**20
        ),
    )(key_grads, router_grads, gain_grads, key_state, router_state, gain_state)


def on_device(
    wide_size,
    key_grads,
    router_grads,
    gain_grads,
    key_master,
    key_first,
    key_second,
    router_master,
    router_first,
    router_second,
    gain_master,
    gain_first,
    gain_second,
):
    key_state = [key_master, key_first, key_second]
    router_state = [router_master, router_first, router_second]
    gain_state = [x.reshape(1, -1) for x in (gain_master, gain_first, gain_second)]
    sums = reduce_grads(
        wide_size, key_grads, router_grads, gain_grads, key_state, router_state, gain_state
    )
    key_new, router_new, gain_new, key_weight, router_weight, gain_weight = update_all(
        sums, key_state, router_state, gain_state
    )
    return (
        *key_new,
        *router_new,
        *[x.reshape(-1) for x in gain_new],
        key_weight.reshape(-1, key_weight.shape[2]),
        router_weight,
        gain_weight.reshape(-1),
    )


def solution(mesh):
    state = (P("narrow", None),) * 3 + (P(None, "narrow"),) * 3 + (P("narrow"),) * 3
    grads = (
        P("wide", "narrow", None, None, None),
        P("wide", "narrow", None, None, None),
        P("wide", "narrow", None, None),
    )
    return jax.shard_map(
        functools.partial(on_device, mesh.shape["wide"]),
        mesh=mesh,
        in_specs=grads + state,
        out_specs=state + (P(), P(), P()),
        check_vma=False,
    )
```

```python
import functools
import math

import jax
import jax.numpy as jnp
from jax import lax
from jax.experimental import pallas as pl
from jax.experimental.pallas import tpu as pltpu
from jax.sharding import PartitionSpec as P

beta_one = 0.9
beta_two = 0.95
step_rate = 0.01
epsilon = 1e-08
bias_one = 1.0 - 0.9**10
bias_two = 1.0 - 0.95**10

LANES = 128
PARTS = 6
HALVED_BITS = 4
F32, BF16 = jnp.float32, jnp.bfloat16


def adamw(master, first_moment, second, gradient, factor, decay_rate):
    scaled = factor * gradient
    first_new = beta_one * first_moment + (1.0 - beta_one) * scaled
    second_new = beta_two * second + (1.0 - beta_two) * scaled * scaled
    root = jnp.sqrt(second_new * (1.0 / bias_two)) + epsilon
    update = first_new * (1.0 / bias_one) / root
    if decay_rate:
        update = update + decay_rate * master
    return (master - step_rate * update, first_new, second_new)


def rows_loop(count, step, body):
    def one(i, carry):
        body(pl.multiple_of(i * step, 16))
        return carry

    lax.fori_loop(0, count // step, one, 0)


def layout(key_shape, router_shape):
    half_rows, half_cols = key_shape[0] // 2, router_shape[1] // 2
    blocks, at = [], 0
    for col in range(0, key_shape[1], LANES):
        blocks.append((at, half_rows, "key", col))
        at += half_rows
    for col in range(0, half_cols, LANES):
        blocks.append((at, router_shape[0], "router", col))
        at += router_shape[0]
    return blocks, at


def part_orders():
    return (("x", 1, 2), (1, 2, "x"), (2, "x", 1)) * (PARTS // 3)


def stage_shapes(part_rows, wide_bits):
    plans = []
    for order in part_orders():
        halves, count, plan = 2, part_rows, []
        for axis in (0,) + order + (3,):
            if axis == "x":
                halves = 1
            else:
                count //= 2
            plan.append((axis, (halves, count, LANES)))
        for axis in range(HALVED_BITS, wide_bits):
            plan.append((axis, (halves, count, LANES)))
        plans.append(plan)
    return plans


def reduce_kernel(
    plans,
    blocks,
    total_rows,
    clip_limit,
    key_ref,
    router_ref,
    gain_ref,
    key_state,
    router_state,
    gain_state,
    packed_out,
    small_out,
    grads,
    gain_grads,
    local,
    acc,
    full,
    gain_val,
    gain_in,
    square_val,
    square_in,
    send_bufs,
    recv_bufs,
    send_sem,
    recv_sem,
    gather_send,
    gather_recv,
    gain_send,
    gain_recv,
    square_send,
    square_recv,
    state,
    gain_mine,
    weight,
    far,
    gain_own,
    gain_new,
    gain_far,
    small,
    load_sem,
    state_sem,
    weight_send,
    weight_recv,
    gain_far_sem,
    out_sem,
):
    wide, narrow = lax.axis_index("wide"), lax.axis_index("narrow")
    stages = len(plans[0])
    part_rows = total_rows // PARTS
    wide_bits = stages - 1
    bit = [(wide // 2**k) % 2 for k in range(wide_bits)]

    def partner(axis):
        if axis == "x":
            return (wide, 1 - narrow)
        return (wide + (1 - 2 * bit[axis]) * 2**axis, narrow)

    diagonal = (partner(3)[0], 1 - narrow)
    friends = [partner(a) for a in ["x"] + list(range(wide_bits))] + [diagonal]
    barrier = pltpu.get_barrier_semaphore()
    for friend in friends:
        pl.semaphore_signal(barrier, inc=1, device_id=friend, device_id_type=pl.DeviceIdType.MESH)
    half_rows, half_cols = key_ref.shape[3] // 2, router_ref.shape[4] // 2
    gain_load = pltpu.make_async_copy(gain_ref.at[0, 0], gain_grads, load_sem.at[0])
    gain_load.start()
    loads = []
    for p in range(PARTS):
        part_loads = []
        for half in range(2):
            for at, count, kind, col in blocks:
                start, stop = max(at, p * part_rows), min(at + count, (p + 1) * part_rows)
                if start >= stop:
                    continue
                first = start - at + (half * half_rows if kind == "key" else 0)
                left = col + (half * half_cols if kind == "router" else 0)
                source = key_ref if kind == "key" else router_ref
                copy = pltpu.make_async_copy(
                    source.at[0, 0, :, pl.ds(first, stop - start), pl.ds(left, LANES)],
                    grads.at[:, half, pl.ds(start, stop - start), :],
                    load_sem.at[1 + len(part_loads) + sum(map(len, loads))],
                )
                copy.start()
                part_loads.append(copy)
        loads.append(part_loads)

    pl.semaphore_wait(barrier, len(friends))

    def remote(src, dst, send, recv, to):
        return pltpu.make_async_remote_copy(
            src_ref=src,
            dst_ref=dst,
            send_sem=send,
            recv_sem=recv,
            device_id=to,
            device_id_type=pl.DeviceIdType.MESH,
        )

    started = []
    gain_copies = []

    def send_gain(stage):
        copy = remote(
            gain_val.at[stage],
            gain_in.at[stage],
            gain_send.at[stage],
            gain_recv.at[stage],
            partner(plans[0][stage][0]),
        )
        copy.start()
        gain_copies.append(copy)

    gain_load.wait()
    gain_local = jnp.sum(gain_grads[...].astype(F32), axis=0, keepdims=True)
    gain_val[0] = gain_local.astype(BF16).astype(F32)
    send_gain(0)
    copies = []
    for p in range(PARTS):
        for load in loads[p]:
            load.wait()
        count = part_rows // 2
        sent = pl.multiple_of(p * part_rows + (1 - bit[0]) * count, 16)
        kept = pl.multiple_of(p * part_rows + bit[0] * count, 16)

        def fill(r, first):
            rows = pl.ds(pl.multiple_of(first + r, 16), 96)
            for half in range(2):
                local[half, rows, :] = grads[0, half, rows, :] + grads[1, half, rows, :]

        rows_loop(count, 96, functools.partial(fill, first=sent))
        copy = remote(
            local.at[:, pl.ds(sent, count), :],
            recv_bufs[p][0],
            send_sem.at[p, 0],
            recv_sem.at[p, 0],
            partner(0),
        )
        copy.start()
        copies.append(copy)
        started.append(copy)
        rows_loop(count, 96, functools.partial(fill, first=kept))

    state_loads = []

    def load_state(source, target):
        copy = pltpu.make_async_copy(source, target, state_sem.at[len(state_loads)])
        copy.start()
        state_loads.append(copy)

    for i in range(3):
        load_state(gain_state[i], gain_mine.at[i])
        for at, count, kind, col in blocks:
            source = key_state[i] if kind == "key" else router_state[i]
            load_state(source.at[:, pl.ds(col, LANES)], state.at[i, pl.ds(at, count), :])

    base = [pl.multiple_of(p * part_rows + bit[0] * (part_rows // 2), 16) for p in range(PARTS)]
    rows_now = [part_rows // 2] * PARTS
    split = [False] * PARTS

    def add(p, stage, half, h, offset, r, step):
        previous = local if stage == 0 else acc
        mine = previous[half, pl.ds(pl.multiple_of(base[p] + offset + r, 16), step), :]
        theirs = recv_bufs[p][stage][h, pl.ds(pl.multiple_of(offset + r, 16), step), :]
        return mine.astype(F32) + theirs.astype(F32)

    for stage in range(1, stages):
        gain_copies[stage - 1].wait_recv()
        gain_val[stage] = gain_val[stage - 1] + gain_in[stage - 1]
        send_gain(stage)
        fresh = []
        for p in range(PARTS):
            axis, shape = plans[p][stage]
            copies[p].wait_recv()
            halves = [(narrow, 0)] if split[p] else [(0, 0), (1, 1)]
            send_buf = send_bufs[p][stage - 1]
            step = min(96, shape[1])
            if axis == "x":
                send_sets, keep_sets = [(1 - narrow, 1 - narrow, 0)], [(narrow, narrow)]
                send_offset = keep_offset = 0
            elif axis < HALVED_BITS:
                send_sets = [(half, h, h) for half, h in halves]
                keep_sets = halves
                send_offset = (1 - bit[axis]) * shape[1]
                keep_offset = bit[axis] * shape[1]
            else:
                send_sets, keep_sets = [(narrow, 0, 0)], []
                send_offset = keep_offset = 0

            def out(r, p=p):
                for half, h, slot in send_sets:
                    value = add(p, stage - 1, half, h, send_offset, r, step)
                    send_buf[slot, pl.ds(r, step), :] = value.astype(BF16)
                    if not keep_sets:
                        rows = pl.ds(pl.multiple_of(base[p] + r, 16), step)
                        acc[half, rows, :] = value.astype(BF16).astype(F32)

            rows_loop(shape[1], step, out)
            copy = remote(
                send_buf,
                recv_bufs[p][stage],
                send_sem.at[p, stage],
                recv_sem.at[p, stage],
                partner(axis),
            )
            copy.start()
            fresh.append(copy)
            started.append(copy)

            def keep(r, p=p):
                for half, h in keep_sets:
                    value = add(p, stage - 1, half, h, keep_offset, r, step)
                    rows = pl.ds(pl.multiple_of(base[p] + keep_offset + r, 16), step)
                    acc[half, rows, :] = value

            if keep_sets:
                rows_loop(shape[1], step, keep)
            if axis == "x":
                split[p] = True
            base[p] = pl.multiple_of(base[p] + keep_offset, 16)
            rows_now[p] = shape[1]
        copies = fresh

    gather_axes = [
        [3] + [a for a in reversed(part_orders()[p]) if a != "x"] + [0] for p in range(PARTS)
    ]
    gathers = []

    def gather(p, stage):
        rows = pl.ds(base[p], rows_now[p])
        axis = gather_axes[p][stage]
        copy = remote(
            full.at[rows, :],
            full.at[rows, :],
            gather_send.at[p, stage],
            gather_recv.at[p, stage],
            partner(axis),
        )
        copy.start()
        started.append(copy)
        base[p] = pl.multiple_of(base[p] - bit[axis] * rows_now[p], 16)
        rows_now[p] = 2 * rows_now[p]
        return copy

    squares = jnp.zeros((8, LANES), F32)
    for p in range(PARTS):
        copies[p].wait_recv()
        count = rows_now[p]
        value = add(p, stages - 1, narrow, 0, 0, 0, count)
        full[pl.ds(base[p], count), :] = value.astype(BF16)
        gathers.append(gather(p, 0))
        squares = squares + jnp.sum((value * value).reshape(count // 8, 8, LANES), axis=0)

    def send_square(source, slot, to):
        copy = remote(
            square_val.at[source],
            square_in.at[slot],
            square_send.at[slot],
            square_recv.at[slot],
            to,
        )
        copy.start()
        started.append(copy)
        return copy

    square_val[0] = squares
    square_copies = [
        send_square(0, 0, partner("x")),
        send_square(0, 1, partner(3)),
        send_square(0, 2, diagonal),
    ]
    gain_copies[stages - 1].wait_recv()
    gain_sum = gain_val[stages - 1] + gain_in[stages - 1]
    gain_val[stages] = gain_sum
    left = pl.multiple_of(narrow * gain_own.shape[1], 128)
    gain_own[...] = gain_val[stages, :, pl.ds(left, gain_own.shape[1])]
    for copy in square_copies:
        copy.wait_recv()
    square_val[1] = (square_val[0] + square_in[0]) + (square_in[1] + square_in[2])
    square_copy = send_square(1, 3, partner(2))
    for p in range(PARTS):
        gathers[p].wait_recv()
        gathers[p] = gather(p, 1)
    for stage in range(2, 4):
        square_copy.wait_recv()
        square_val[stage] = square_val[stage - 1] + square_in[stage + 1]
        square_copy = send_square(stage, stage + 2, partner((1, 0)[stage - 2]))
    for copy in state_loads:
        copy.wait()
    square_copy.wait_recv()
    total = jnp.sum(square_val[3] + square_in[5]) + jnp.sum(gain_sum * gain_sum)
    total = jnp.full((8, 128), total, F32)
    gain_tiles = gain_own.shape[1] // 128
    small[2 * gain_tiles :, :] = clip_limit / jnp.maximum(jnp.sqrt(total), clip_limit)
    factor = small[2 * gain_tiles : 2 * gain_tiles + 1, 0:1]

    def forward(p, hop, start, axis):
        block = far.at[pl.ds(start, quarter_rows), :]
        copy = remote(block, block, weight_send.at[hop, p], weight_recv.at[hop, p], partner(axis))
        copy.start()
        started.append(copy)
        return copy

    quarter_rows = part_rows // 4
    held, across = [], []
    for p in range(PARTS):
        gathers[p].wait_recv()
        start = base[p]
        held.append(start)
        gathers[p] = gather(p, 2)

        def renew(r, p=p, start=start):
            rows = pl.ds(pl.multiple_of(start + r, 16), 64)
            old = [state[i, rows, :] for i in range(3)]
            new = adamw(*old, full[rows, :].astype(F32), factor, 0.1)[0]
            weight[p, pl.ds(r, 64), :] = new.astype(BF16)

        rows_loop(quarter_rows, 64, renew)
        copy = remote(
            weight.at[p],
            far.at[pl.ds(start, quarter_rows), :],
            weight_send.at[0, p],
            weight_recv.at[0, p],
            partner("x"),
        )
        copy.start()
        started.append(copy)
        across.append(copy)
    gain_new[...] = adamw(
        gain_mine[0], gain_mine[1], gain_mine[2], gain_own[...], factor, 0.0
    )[0]
    gain_copy = remote(gain_new, gain_far, gain_far_sem.at[0], gain_far_sem.at[1], partner("x"))
    gain_copy.start()

    beside, own, other = [], [], []
    for p in range(PARTS):
        gathers[p].wait_recv()
        gathers[p] = gather(p, 3)
        across[p].wait_recv()
        beside.append(forward(p, 1, held[p], gather_axes[p][2]))
        own.append(forward(p, 2, held[p], 0))
    for p in range(PARTS):
        beside[p].wait_recv()
        step = (1 - 2 * bit[gather_axes[p][2]]) * quarter_rows
        other.append(forward(p, 3, pl.multiple_of(held[p] + step, 16), 0))

    out_copies = []

    def leave(source, target):
        copy = pltpu.make_async_copy(source, target, out_sem.at[len(out_copies)])
        copy.start()
        out_copies.append(copy)

    def leave_packed(source, place):
        keys = [at for at, _, kind, _ in blocks if kind == "key"]
        for i, at in enumerate(keys):
            leave(source.at[pl.ds(at, half_rows), :], packed_out.at[place, i])
        at = len(keys) * half_rows
        rest = total_rows - at
        leave(
            source.at[pl.ds(at, rest), :], packed_out.at[place, len(keys), pl.ds(0, rest), :]
        )

    for copy in gathers:
        copy.wait_recv()
    leave_packed(full, 0)
    gain_copy.wait_recv()
    for j in range(gain_tiles):
        cols = slice(128 * j, 128 * (j + 1))
        small[j : j + 1, :] = gain_own[:, cols]
        small[gain_tiles + j : gain_tiles + j + 1, :] = gain_far[:, cols]
    leave(small, small_out.at[pl.ds(0, small.shape[0]), :])
    for copy in own + other:
        copy.wait_recv()
    leave_packed(far, 1)
    for copy in started + gain_copies + [gain_copy]:
        copy.wait_send()
    for copy in out_copies:
        copy.wait()


def update_kernel(
    packed,
    small_in,
    key_state,
    router_state,
    gain_state,
    key_new,
    router_new,
    gain_new,
    key_weight,
    router_weight,
    gain_weight,
    keys,
    routers,
    small,
    gain_rows,
    key_sem,
    other_sem,
):
    narrow, at = lax.axis_index("narrow"), pl.program_id(0)
    steps = pl.num_programs(0)
    blocks, block_rows, experts = keys.shape[1], key_new[0].shape[0], router_new[0].shape[0]
    gain_tiles = gain_rows.shape[0] // 2

    def key_copy(i):
        rows = pl.ds(pl.multiple_of(i * block_rows, 16), block_rows)
        return pltpu.make_async_copy(
            packed.at[:, pl.ds(0, blocks), rows, :], keys.at[:, :, rows, :], key_sem.at[i]
        )

    other_copies = [
        pltpu.make_async_copy(
            small_in.at[pl.ds(0, small.shape[0]), :], small, other_sem.at[0]
        ),
        pltpu.make_async_copy(
            packed.at[:, blocks, pl.ds(0, routers.shape[1]), :], routers, other_sem.at[1]
        ),
    ]

    @pl.when(at == 0)
    def _():
        for copy in other_copies:
            copy.start()
        for i in range(keys.shape[2] // block_rows):
            key_copy(i).start()
        for copy in other_copies:
            copy.wait()

    factor = small[2 * gain_tiles : 2 * gain_tiles + 1, 0:1]

    def update(state, gradient, decay_rate, new, rows, cols):
        old = [ref[rows, cols] for ref in state]
        values = adamw(*old, gradient.astype(F32), factor, decay_rate)
        for ref, value in zip(new, values):
            ref[rows, cols] = value
        return values[0]

    @pl.when(at == 0)
    def _():
        for j in range(gain_tiles):
            cols = slice(128 * j, 128 * (j + 1))
            value = update(
                gain_state, small[j : j + 1, :], 0.0, gain_new, slice(0, 1), cols
            )
            gain_rows[pl.ds(narrow * gain_tiles + j, 1), :] = value
            other = small[gain_tiles + j : gain_tiles + j + 1, :]
            gain_rows[pl.ds((1 - narrow) * gain_tiles + j, 1), :] = other
        gain_weight[...] = gain_rows[...].astype(BF16)

    rows = pl.ds(pl.multiple_of(at * experts, 16), experts)
    value = update(
        router_state, routers[0, rows, :], 0.1, router_new, slice(None), slice(None)
    )

    def columns(n):
        return pl.ds(pl.multiple_of((n * steps + at) * LANES, 128), LANES)

    router_weight[:, columns(narrow)] = value.astype(BF16)
    router_weight[:, columns(1 - narrow)] = routers[1, rows, :]

    key_copy(at).wait()
    rows = pl.ds(pl.multiple_of(at * block_rows, 16), block_rows)
    for j in range(blocks):
        cols = slice(LANES * j, LANES * (j + 1))
        value = update(key_state, keys[0, j, rows, :], 0.1, key_new, slice(None), cols)
        key_weight[narrow, :, cols] = value.astype(BF16)
        key_weight[1 - narrow, :, cols] = keys[1, j, rows, :]


def update_all(packed, small, key_state, router_state, gain_state):
    (rows, width), (experts, cols) = key_state[0].shape, router_state[0].shape
    gain = gain_state[0].shape[1]
    steps = cols // LANES
    key_spec = pl.BlockSpec((rows // steps, width), lambda i: (i, 0))
    router_spec = pl.BlockSpec((experts, LANES), lambda i: (0, i))
    gain_spec = pl.BlockSpec((1, gain), lambda i: (0, 0))
    shape = jax.ShapeDtypeStruct
    return pl.pallas_call(
        update_kernel,
        grid=(steps,),
        out_shape=(
            [shape((rows, width), F32)] * 3,
            [shape((experts, cols), F32)] * 3,
            [shape((1, gain), F32)] * 3,
            shape((2, rows, width), BF16),
            shape((experts, 2 * cols), BF16),
            shape((2 * gain // 128, 128), BF16),
        ),
        in_specs=[pl.BlockSpec(memory_space=pltpu.HBM)] * 2
        + [[key_spec] * 3, [router_spec] * 3, [gain_spec] * 3],
        out_specs=(
            [key_spec] * 3,
            [router_spec] * 3,
            [gain_spec] * 3,
            pl.BlockSpec((2, rows // steps, width), lambda i: (0, i, 0)),
            pl.BlockSpec((experts, 2 * cols), lambda i: (0, 0)),
            pl.BlockSpec((2 * gain // 128, 128), lambda i: (0, 0)),
        ),
        scratch_shapes=[
            pltpu.VMEM((2, width // LANES, rows, LANES), BF16),
            pltpu.VMEM((2, experts * steps, LANES), BF16),
            pltpu.VMEM((2 * gain // 128 + 8, 128), F32),
            pltpu.VMEM((2 * gain // 128, 128), F32),
            pltpu.SemaphoreType.DMA((steps,)),
            pltpu.SemaphoreType.DMA((2,)),
        ],
        compiler_params=pltpu.CompilerParams(vmem_limit_bytes=46 * 2**20),
    )(packed, small, key_state, router_state, gain_state)


def reduce_grads(
    wide_size, key_grads, router_grads, gain_grads, key_state, router_state, gain_state
):
    key_shape, router_shape = key_grads.shape[3:], router_grads.shape[3:]
    gain_size = gain_grads.shape[3]
    blocks, total_rows = layout(key_shape, router_shape)
    wide_bits = wide_size.bit_length() - 1
    plans = stage_shapes(total_rows // PARTS, wide_bits)
    stages = len(plans[0])
    count = math.prod(key_shape) + math.prod(router_shape) + gain_size
    hbm = pl.BlockSpec(memory_space=pl.ANY)
    half_rows, width = key_shape[0] // 2, key_shape[1]
    return pl.pallas_call(
        functools.partial(
            reduce_kernel, plans, blocks, total_rows, 0.5 * math.sqrt(count)
        ),
        out_shape=(
            jax.ShapeDtypeStruct((2, 4 * (width // LANES), half_rows, LANES), BF16),
            jax.ShapeDtypeStruct((16 * half_rows, 128), F32),
        ),
        in_specs=[hbm] * 3 + [[hbm] * 3] * 3,
        out_specs=(hbm, hbm),
        scratch_shapes=[
            pltpu.VMEM((2, 2, total_rows, LANES), BF16),
            pltpu.VMEM((2, gain_size), BF16),
            pltpu.VMEM((2, total_rows, LANES), BF16),
            pltpu.VMEM((2, total_rows, LANES), F32),
            pltpu.VMEM((total_rows, LANES), BF16),
            pltpu.VMEM((stages + 1, 1, gain_size), F32),
            pltpu.VMEM((stages, 1, gain_size), F32),
            pltpu.VMEM((5, 8, LANES), F32),
            pltpu.VMEM((6, 8, LANES), F32),
            [[pltpu.VMEM(shape, BF16) for _, shape in plan[1:]] for plan in plans],
            [[pltpu.VMEM(shape, BF16) for _, shape in plan] for plan in plans],
            pltpu.SemaphoreType.DMA((PARTS, stages)),
            pltpu.SemaphoreType.DMA((PARTS, stages)),
            pltpu.SemaphoreType.DMA((PARTS, 4)),
            pltpu.SemaphoreType.DMA((PARTS, 4)),
            pltpu.SemaphoreType.DMA((stages,)),
            pltpu.SemaphoreType.DMA((stages,)),
            pltpu.SemaphoreType.DMA((6,)),
            pltpu.SemaphoreType.DMA((6,)),
            pltpu.VMEM((3, total_rows, LANES), F32),
            pltpu.VMEM((3, 1, gain_size // 2), F32),
            pltpu.VMEM((PARTS, total_rows // PARTS // 4, LANES), BF16),
            pltpu.VMEM((total_rows, LANES), BF16),
            pltpu.VMEM((1, gain_size // 2), F32),
            pltpu.VMEM((1, gain_size // 2), F32),
            pltpu.VMEM((1, gain_size // 2), F32),
            pltpu.VMEM((gain_size // 128 + 8, 128), F32),
            pltpu.SemaphoreType.DMA((2 * (len(blocks) + PARTS) + 1,)),
            pltpu.SemaphoreType.DMA((3 * (len(blocks) + 1),)),
            pltpu.SemaphoreType.DMA((4, PARTS)),
            pltpu.SemaphoreType.DMA((4, PARTS)),
            pltpu.SemaphoreType.DMA((2,)),
            pltpu.SemaphoreType.DMA((2 * (width // LANES + 1) + 1,)),
        ],
        compiler_params=pltpu.CompilerParams(
            collective_id=0, has_side_effects=True, vmem_limit_bytes=56 * 2**20
        ),
    )(key_grads, router_grads, gain_grads, key_state, router_state, gain_state)


def on_device(
    wide_size,
    key_grads,
    router_grads,
    gain_grads,
    key_master,
    key_first,
    key_second,
    router_master,
    router_first,
    router_second,
    gain_master,
    gain_first,
    gain_second,
):
    key_state = [key_master, key_first, key_second]
    router_state = [router_master, router_first, router_second]
    gain_state = [x.reshape(1, -1) for x in (gain_master, gain_first, gain_second)]
    sums = reduce_grads(
        wide_size, key_grads, router_grads, gain_grads, key_state, router_state, gain_state
    )
    key_new, router_new, gain_new, key_weight, router_weight, gain_weight = update_all(
        *sums, key_state, router_state, gain_state
    )
    return (
        *key_new,
        *router_new,
        *[x.reshape(-1) for x in gain_new],
        key_weight.reshape(-1, key_weight.shape[2]),
        router_weight,
        gain_weight.reshape(-1),
    )


def solution(mesh):
    state = (P("narrow", None),) * 3 + (P(None, "narrow"),) * 3 + (P("narrow"),) * 3
    grads = (
        P("wide", "narrow", None, None, None),
        P("wide", "narrow", None, None, None),
        P("wide", "narrow", None, None),
    )
    return jax.shard_map(
        functools.partial(on_device, mesh.shape["wide"]),
        mesh=mesh,
        in_specs=grads + state,
        out_specs=state + (P(), P(), P()),
        check_vma=False,
    )
```

```python
import functools
import math

import jax
import jax.numpy as jnp
from jax import lax
from jax.experimental import pallas as pl
from jax.experimental.pallas import tpu as pltpu
from jax.sharding import PartitionSpec as P

beta_one = 0.9
beta_two = 0.95
step_rate = 0.01
epsilon = 1e-08
bias_one = 1.0 - 0.9**10
bias_two = 1.0 - 0.95**10

LANES = 128
PARTS = 6
HALVED_BITS = 4
F32, BF16 = jnp.float32, jnp.bfloat16


def adamw(master, first_moment, second, gradient, factor, decay_rate):
    scaled = factor * gradient
    first_new = beta_one * first_moment + (1.0 - beta_one) * scaled
    second_new = beta_two * second + (1.0 - beta_two) * scaled * scaled
    spread = second_new * (1.0 / bias_two)
    root = spread * lax.rsqrt(spread) + epsilon
    update = first_new * (1.0 / bias_one) / root
    if decay_rate:
        update = update + decay_rate * master
    return (master - step_rate * update, first_new, second_new)


def rows_loop(count, step, body):
    def one(i, carry):
        body(pl.multiple_of(i * step, 16))
        return carry

    lax.fori_loop(0, count // step, one, 0)


def layout(key_shape, router_shape):
    half_rows, half_cols = key_shape[0] // 2, router_shape[1] // 2
    blocks, at = [], 0
    for col in range(0, key_shape[1], LANES):
        blocks.append((at, half_rows, "key", col))
        at += half_rows
    for col in range(0, half_cols, LANES):
        blocks.append((at, router_shape[0], "router", col))
        at += router_shape[0]
    return blocks, at


def part_orders():
    return (("x", 1, 2), (1, 2, "x"), (2, "x", 1)) * (PARTS // 3)


def stage_shapes(part_rows, wide_bits):
    plans = []
    for order in part_orders():
        halves, count, plan = 2, part_rows, []
        for axis in (0,) + order + (3,):
            if axis == "x":
                halves = 1
            else:
                count //= 2
            plan.append((axis, (halves, count, LANES)))
        for axis in range(HALVED_BITS, wide_bits):
            plan.append((axis, (halves, count, LANES)))
        plans.append(plan)
    return plans


def reduce_kernel(
    plans,
    blocks,
    total_rows,
    clip_limit,
    key_ref,
    router_ref,
    gain_ref,
    key_state,
    router_state,
    gain_state,
    packed_out,
    small_out,
    grads,
    gain_grads,
    local,
    acc,
    full,
    gain_val,
    gain_in,
    square_val,
    square_in,
    send_bufs,
    recv_bufs,
    send_sem,
    recv_sem,
    gather_send,
    gather_recv,
    gain_send,
    gain_recv,
    square_send,
    square_recv,
    state,
    gain_mine,
    weight,
    far,
    gain_own,
    gain_new,
    gain_far,
    small,
    load_sem,
    state_sem,
    weight_send,
    weight_recv,
    gain_far_sem,
    out_sem,
):
    wide, narrow = lax.axis_index("wide"), lax.axis_index("narrow")
    stages = len(plans[0])
    part_rows = total_rows // PARTS
    wide_bits = stages - 1
    bit = [(wide // 2**k) % 2 for k in range(wide_bits)]

    def partner(axis):
        if axis == "x":
            return (wide, 1 - narrow)
        return (wide + (1 - 2 * bit[axis]) * 2**axis, narrow)

    diagonal = (partner(3)[0], 1 - narrow)
    friends = [partner(a) for a in ["x"] + list(range(wide_bits))] + [diagonal]
    barrier = pltpu.get_barrier_semaphore()
    for friend in friends:
        pl.semaphore_signal(barrier, inc=1, device_id=friend, device_id_type=pl.DeviceIdType.MESH)
    half_rows, half_cols = key_ref.shape[3] // 2, router_ref.shape[4] // 2
    gain_load = pltpu.make_async_copy(gain_ref.at[0, 0], gain_grads, load_sem.at[0])
    gain_load.start()
    loads = []
    for p in range(PARTS):
        part_loads = []
        for half in range(2):
            for at, count, kind, col in blocks:
                start, stop = max(at, p * part_rows), min(at + count, (p + 1) * part_rows)
                if start >= stop:
                    continue
                first = start - at + (half * half_rows if kind == "key" else 0)
                left = col + (half * half_cols if kind == "router" else 0)
                source = key_ref if kind == "key" else router_ref
                copy = pltpu.make_async_copy(
                    source.at[0, 0, :, pl.ds(first, stop - start), pl.ds(left, LANES)],
                    grads.at[:, half, pl.ds(start, stop - start), :],
                    load_sem.at[1 + len(part_loads) + sum(map(len, loads))],
                )
                copy.start()
                part_loads.append(copy)
        loads.append(part_loads)

    pl.semaphore_wait(barrier, len(friends))

    def remote(src, dst, send, recv, to):
        return pltpu.make_async_remote_copy(
            src_ref=src,
            dst_ref=dst,
            send_sem=send,
            recv_sem=recv,
            device_id=to,
            device_id_type=pl.DeviceIdType.MESH,
        )

    started = []
    gain_copies = []

    def send_gain(stage):
        copy = remote(
            gain_val.at[stage],
            gain_in.at[stage],
            gain_send.at[stage],
            gain_recv.at[stage],
            partner(plans[0][stage][0]),
        )
        copy.start()
        gain_copies.append(copy)

    gain_load.wait()
    gain_local = jnp.sum(gain_grads[...].astype(F32), axis=0, keepdims=True)
    gain_val[0] = gain_local.astype(BF16).astype(F32)
    send_gain(0)
    copies = []
    for p in range(PARTS):
        for load in loads[p]:
            load.wait()
        count = part_rows // 2
        sent = pl.multiple_of(p * part_rows + (1 - bit[0]) * count, 16)
        kept = pl.multiple_of(p * part_rows + bit[0] * count, 16)

        def fill(r, first):
            rows = pl.ds(pl.multiple_of(first + r, 16), 96)
            for half in range(2):
                local[half, rows, :] = grads[0, half, rows, :] + grads[1, half, rows, :]

        rows_loop(count, 96, functools.partial(fill, first=sent))
        copy = remote(
            local.at[:, pl.ds(sent, count), :],
            recv_bufs[p][0],
            send_sem.at[p, 0],
            recv_sem.at[p, 0],
            partner(0),
        )
        copy.start()
        copies.append(copy)
        started.append(copy)
        rows_loop(count, 96, functools.partial(fill, first=kept))

    state_loads = []

    def load_state(source, target):
        copy = pltpu.make_async_copy(source, target, state_sem.at[len(state_loads)])
        copy.start()
        state_loads.append(copy)

    base = [pl.multiple_of(p * part_rows + bit[0] * (part_rows // 2), 16) for p in range(PARTS)]
    rows_now = [part_rows // 2] * PARTS
    split = [False] * PARTS

    def add(p, stage, half, h, start, offset, r, step):
        previous = local if stage == 0 else acc
        mine = previous[half, pl.ds(pl.multiple_of(start + offset + r, 16), step), :]
        theirs = recv_bufs[p][stage][h, pl.ds(pl.multiple_of(offset + r, 16), step), :]
        return mine.astype(F32) + theirs.astype(F32)

    for stage in range(1, stages):
        if stage == 2:
            for i in range(3):
                load_state(gain_state[i], gain_mine.at[i])
                for at, count, kind, col in blocks:
                    source = key_state[i] if kind == "key" else router_state[i]
                    load_state(source.at[:, pl.ds(col, LANES)], state.at[i, pl.ds(at, count), :])
        gain_copies[stage - 1].wait_recv()
        gain_val[stage] = gain_val[stage - 1] + gain_in[stage - 1]
        send_gain(stage)
        fresh, pending = [], []
        for p in range(PARTS):
            axis, shape = plans[p][stage]
            copies[p].wait_recv()
            halves = [(narrow, 0)] if split[p] else [(0, 0), (1, 1)]
            send_buf = send_bufs[p][stage - 1]
            step = min(96, shape[1])
            if axis == "x":
                send_sets, keep_sets = [(1 - narrow, 1 - narrow, 0)], [(narrow, narrow)]
                send_offset = keep_offset = 0
            elif axis < HALVED_BITS:
                send_sets = [(half, h, h) for half, h in halves]
                keep_sets = halves
                send_offset = (1 - bit[axis]) * shape[1]
                keep_offset = bit[axis] * shape[1]
            else:
                send_sets, keep_sets = [(narrow, 0, 0)], []
                send_offset = keep_offset = 0

            def out(r, p=p):
                for half, h, slot in send_sets:
                    value = add(p, stage - 1, half, h, base[p], send_offset, r, step)
                    send_buf[slot, pl.ds(r, step), :] = value.astype(BF16)
                    if not keep_sets:
                        rows = pl.ds(pl.multiple_of(base[p] + r, 16), step)
                        acc[half, rows, :] = value.astype(BF16).astype(F32)

            rows_loop(shape[1], step, out)
            copy = remote(
                send_buf,
                recv_bufs[p][stage],
                send_sem.at[p, stage],
                recv_sem.at[p, stage],
                partner(axis),
            )
            copy.start()
            fresh.append(copy)
            started.append(copy)

            def keep(
                r, p=p, sets=keep_sets, start=base[p], offset=keep_offset, step=step
            ):
                for half, h in sets:
                    value = add(p, stage - 1, half, h, start, offset, r, step)
                    rows = pl.ds(pl.multiple_of(start + offset + r, 16), step)
                    acc[half, rows, :] = value

            if keep_sets:
                pending.append((shape[1], step, keep))
            if axis == "x":
                split[p] = True
            base[p] = pl.multiple_of(base[p] + keep_offset, 16)
            rows_now[p] = shape[1]
            if p % 3 == 2:
                for job in pending:
                    rows_loop(*job)
                pending = []
        copies = fresh

    gather_axes = [
        [3] + [a for a in reversed(part_orders()[p]) if a != "x"] + [0] for p in range(PARTS)
    ]
    gathers = []

    def gather(p, stage):
        rows = pl.ds(base[p], rows_now[p])
        axis = gather_axes[p][stage]
        copy = remote(
            full.at[rows, :],
            full.at[rows, :],
            gather_send.at[p, stage],
            gather_recv.at[p, stage],
            partner(axis),
        )
        copy.start()
        started.append(copy)
        base[p] = pl.multiple_of(base[p] - bit[axis] * rows_now[p], 16)
        rows_now[p] = 2 * rows_now[p]
        return copy

    squares = jnp.zeros((8, LANES), F32)
    for p in range(PARTS):
        copies[p].wait_recv()
        count = rows_now[p]
        value = add(p, stages - 1, narrow, 0, base[p], 0, 0, count)
        full[pl.ds(base[p], count), :] = value.astype(BF16)
        gathers.append(gather(p, 0))
        squares = squares + jnp.sum((value * value).reshape(count // 8, 8, LANES), axis=0)

    def send_square(source, slot, to):
        copy = remote(
            square_val.at[source],
            square_in.at[slot],
            square_send.at[slot],
            square_recv.at[slot],
            to,
        )
        copy.start()
        started.append(copy)
        return copy

    square_val[0] = squares
    square_copies = [
        send_square(0, 0, partner("x")),
        send_square(0, 1, partner(3)),
        send_square(0, 2, diagonal),
    ]
    gain_copies[stages - 1].wait_recv()
    gain_sum = gain_val[stages - 1] + gain_in[stages - 1]
    gain_val[stages] = gain_sum
    left = pl.multiple_of(narrow * gain_own.shape[1], 128)
    gain_own[...] = gain_val[stages, :, pl.ds(left, gain_own.shape[1])]
    for copy in square_copies:
        copy.wait_recv()
    square_val[1] = (square_val[0] + square_in[0]) + (square_in[1] + square_in[2])
    square_copy = send_square(1, 3, partner(2))
    for p in range(PARTS):
        gathers[p].wait_recv()
        gathers[p] = gather(p, 1)
    for stage in range(2, 4):
        square_copy.wait_recv()
        square_val[stage] = square_val[stage - 1] + square_in[stage + 1]
        square_copy = send_square(stage, stage + 2, partner((1, 0)[stage - 2]))
    for copy in state_loads:
        copy.wait()
    square_copy.wait_recv()
    total = jnp.sum(square_val[3] + square_in[5]) + jnp.sum(gain_sum * gain_sum)
    total = jnp.full((8, 128), total, F32)
    gain_tiles = gain_own.shape[1] // 128
    small[2 * gain_tiles :, :] = clip_limit / jnp.maximum(jnp.sqrt(total), clip_limit)
    factor = small[2 * gain_tiles : 2 * gain_tiles + 1, 0:1]

    def forward(p, hop, start, axis):
        block = far.at[pl.ds(start, quarter_rows), :]
        copy = remote(block, block, weight_send.at[hop, p], weight_recv.at[hop, p], partner(axis))
        copy.start()
        started.append(copy)
        return copy

    quarter_rows = part_rows // 4
    held, across = [], []
    for p in range(PARTS):
        gathers[p].wait_recv()
        start = base[p]
        held.append(start)
        gathers[p] = gather(p, 2)

        def renew(r, p=p, start=start):
            rows = pl.ds(pl.multiple_of(start + r, 16), 64)
            old = [state[i, rows, :] for i in range(3)]
            new = adamw(*old, full[rows, :].astype(F32), factor, 0.1)[0]
            weight[p, pl.ds(r, 64), :] = new.astype(BF16)

        rows_loop(quarter_rows, 64, renew)
        copy = remote(
            weight.at[p],
            far.at[pl.ds(start, quarter_rows), :],
            weight_send.at[0, p],
            weight_recv.at[0, p],
            partner("x"),
        )
        copy.start()
        started.append(copy)
        across.append(copy)
    gain_new[...] = adamw(
        gain_mine[0], gain_mine[1], gain_mine[2], gain_own[...], factor, 0.0
    )[0]
    gain_copy = remote(gain_new, gain_far, gain_far_sem.at[0], gain_far_sem.at[1], partner("x"))
    gain_copy.start()

    beside, own, other = [], [], []
    for p in range(PARTS):
        gathers[p].wait_recv()
        gathers[p] = gather(p, 3)
        across[p].wait_recv()
        beside.append(forward(p, 1, held[p], gather_axes[p][2]))
        own.append(forward(p, 2, held[p], 0))
    for p in range(PARTS):
        beside[p].wait_recv()
        step = (1 - 2 * bit[gather_axes[p][2]]) * quarter_rows
        other.append(forward(p, 3, pl.multiple_of(held[p] + step, 16), 0))

    out_copies = []

    def leave(source, target):
        copy = pltpu.make_async_copy(source, target, out_sem.at[len(out_copies)])
        copy.start()
        out_copies.append(copy)

    def leave_packed(source, place):
        keys = [at for at, _, kind, _ in blocks if kind == "key"]
        for i, at in enumerate(keys):
            leave(source.at[pl.ds(at, half_rows), :], packed_out.at[place, i])
        at = len(keys) * half_rows
        rest = total_rows - at
        leave(
            source.at[pl.ds(at, rest), :], packed_out.at[place, len(keys), pl.ds(0, rest), :]
        )

    for copy in gathers:
        copy.wait_recv()
    leave_packed(full, 0)
    gain_copy.wait_recv()
    for j in range(gain_tiles):
        cols = slice(128 * j, 128 * (j + 1))
        small[j : j + 1, :] = gain_own[:, cols]
        small[gain_tiles + j : gain_tiles + j + 1, :] = gain_far[:, cols]
    leave(small, small_out.at[pl.ds(0, small.shape[0]), :])
    for copy in own + other:
        copy.wait_recv()
    leave_packed(far, 1)
    for copy in started + gain_copies + [gain_copy]:
        copy.wait_send()
    for copy in out_copies:
        copy.wait()


def update_kernel(
    packed,
    small_in,
    key_state,
    router_state,
    gain_state,
    key_new,
    router_new,
    gain_new,
    key_weight,
    router_weight,
    gain_weight,
    keys,
    routers,
    small,
    gain_rows,
    key_sem,
    other_sem,
):
    narrow, at = lax.axis_index("narrow"), pl.program_id(0)
    steps = pl.num_programs(0)
    blocks, block_rows, experts = keys.shape[1], key_new[0].shape[0], router_new[0].shape[0]
    gain_tiles = gain_rows.shape[0] // 2

    def key_copy(i):
        rows = pl.ds(pl.multiple_of(i * block_rows, 16), block_rows)
        return pltpu.make_async_copy(
            packed.at[:, pl.ds(0, blocks), rows, :], keys.at[:, :, rows, :], key_sem.at[i]
        )

    other_copies = [
        pltpu.make_async_copy(
            small_in.at[pl.ds(0, small.shape[0]), :], small, other_sem.at[0]
        ),
        pltpu.make_async_copy(
            packed.at[:, blocks, pl.ds(0, routers.shape[1]), :], routers, other_sem.at[1]
        ),
    ]

    @pl.when(at == 0)
    def _():
        for copy in other_copies:
            copy.start()
        for i in range(keys.shape[2] // block_rows):
            key_copy(i).start()
        for copy in other_copies:
            copy.wait()

    factor = small[2 * gain_tiles : 2 * gain_tiles + 1, 0:1]

    def update(state, gradient, decay_rate, new, rows, cols):
        old = [ref[rows, cols] for ref in state]
        values = adamw(*old, gradient.astype(F32), factor, decay_rate)
        for ref, value in zip(new, values):
            ref[rows, cols] = value
        return values[0]

    @pl.when(at == 0)
    def _():
        for j in range(gain_tiles):
            cols = slice(128 * j, 128 * (j + 1))
            value = update(
                gain_state, small[j : j + 1, :], 0.0, gain_new, slice(0, 1), cols
            )
            gain_rows[pl.ds(narrow * gain_tiles + j, 1), :] = value
            other = small[gain_tiles + j : gain_tiles + j + 1, :]
            gain_rows[pl.ds((1 - narrow) * gain_tiles + j, 1), :] = other
        gain_weight[...] = gain_rows[...].astype(BF16)

    rows = pl.ds(pl.multiple_of(at * experts, 16), experts)
    value = update(
        router_state, routers[0, rows, :], 0.1, router_new, slice(None), slice(None)
    )

    def columns(n):
        return pl.ds(pl.multiple_of((n * steps + at) * LANES, 128), LANES)

    router_weight[:, columns(narrow)] = value.astype(BF16)
    router_weight[:, columns(1 - narrow)] = routers[1, rows, :]

    key_copy(at).wait()
    rows = pl.ds(pl.multiple_of(at * block_rows, 16), block_rows)
    for j in range(blocks):
        cols = slice(LANES * j, LANES * (j + 1))
        value = update(key_state, keys[0, j, rows, :], 0.1, key_new, slice(None), cols)
        key_weight[narrow, :, cols] = value.astype(BF16)
        key_weight[1 - narrow, :, cols] = keys[1, j, rows, :]


def update_all(packed, small, key_state, router_state, gain_state):
    (rows, width), (experts, cols) = key_state[0].shape, router_state[0].shape
    gain = gain_state[0].shape[1]
    steps = cols // LANES
    key_spec = pl.BlockSpec((rows // steps, width), lambda i: (i, 0))
    router_spec = pl.BlockSpec((experts, LANES), lambda i: (0, i))
    gain_spec = pl.BlockSpec((1, gain), lambda i: (0, 0))
    shape = jax.ShapeDtypeStruct
    return pl.pallas_call(
        update_kernel,
        grid=(steps,),
        out_shape=(
            [shape((rows, width), F32)] * 3,
            [shape((experts, cols), F32)] * 3,
            [shape((1, gain), F32)] * 3,
            shape((2, rows, width), BF16),
            shape((experts, 2 * cols), BF16),
            shape((2 * gain // 128, 128), BF16),
        ),
        in_specs=[pl.BlockSpec(memory_space=pltpu.HBM)] * 2
        + [[key_spec] * 3, [router_spec] * 3, [gain_spec] * 3],
        out_specs=(
            [key_spec] * 3,
            [router_spec] * 3,
            [gain_spec] * 3,
            pl.BlockSpec((2, rows // steps, width), lambda i: (0, i, 0)),
            pl.BlockSpec((experts, 2 * cols), lambda i: (0, 0)),
            pl.BlockSpec((2 * gain // 128, 128), lambda i: (0, 0)),
        ),
        scratch_shapes=[
            pltpu.VMEM((2, width // LANES, rows, LANES), BF16),
            pltpu.VMEM((2, experts * steps, LANES), BF16),
            pltpu.VMEM((2 * gain // 128 + 8, 128), F32),
            pltpu.VMEM((2 * gain // 128, 128), F32),
            pltpu.SemaphoreType.DMA((steps,)),
            pltpu.SemaphoreType.DMA((2,)),
        ],
        compiler_params=pltpu.CompilerParams(vmem_limit_bytes=46 * 2**20),
    )(packed, small, key_state, router_state, gain_state)


def reduce_grads(
    wide_size, key_grads, router_grads, gain_grads, key_state, router_state, gain_state
):
    key_shape, router_shape = key_grads.shape[3:], router_grads.shape[3:]
    gain_size = gain_grads.shape[3]
    blocks, total_rows = layout(key_shape, router_shape)
    wide_bits = wide_size.bit_length() - 1
    plans = stage_shapes(total_rows // PARTS, wide_bits)
    stages = len(plans[0])
    count = math.prod(key_shape) + math.prod(router_shape) + gain_size
    hbm = pl.BlockSpec(memory_space=pl.ANY)
    half_rows, width = key_shape[0] // 2, key_shape[1]
    return pl.pallas_call(
        functools.partial(
            reduce_kernel, plans, blocks, total_rows, 0.5 * math.sqrt(count)
        ),
        out_shape=(
            jax.ShapeDtypeStruct((2, 4 * (width // LANES), half_rows, LANES), BF16),
            jax.ShapeDtypeStruct((16 * half_rows, 128), F32),
        ),
        in_specs=[hbm] * 3 + [[hbm] * 3] * 3,
        out_specs=(hbm, hbm),
        scratch_shapes=[
            pltpu.VMEM((2, 2, total_rows, LANES), BF16),
            pltpu.VMEM((2, gain_size), BF16),
            pltpu.VMEM((2, total_rows, LANES), BF16),
            pltpu.VMEM((2, total_rows, LANES), F32),
            pltpu.VMEM((total_rows, LANES), BF16),
            pltpu.VMEM((stages + 1, 1, gain_size), F32),
            pltpu.VMEM((stages, 1, gain_size), F32),
            pltpu.VMEM((5, 8, LANES), F32),
            pltpu.VMEM((6, 8, LANES), F32),
            [[pltpu.VMEM(shape, BF16) for _, shape in plan[1:]] for plan in plans],
            [[pltpu.VMEM(shape, BF16) for _, shape in plan] for plan in plans],
            pltpu.SemaphoreType.DMA((PARTS, stages)),
            pltpu.SemaphoreType.DMA((PARTS, stages)),
            pltpu.SemaphoreType.DMA((PARTS, 4)),
            pltpu.SemaphoreType.DMA((PARTS, 4)),
            pltpu.SemaphoreType.DMA((stages,)),
            pltpu.SemaphoreType.DMA((stages,)),
            pltpu.SemaphoreType.DMA((6,)),
            pltpu.SemaphoreType.DMA((6,)),
            pltpu.VMEM((3, total_rows, LANES), F32),
            pltpu.VMEM((3, 1, gain_size // 2), F32),
            pltpu.VMEM((PARTS, total_rows // PARTS // 4, LANES), BF16),
            pltpu.VMEM((total_rows, LANES), BF16),
            pltpu.VMEM((1, gain_size // 2), F32),
            pltpu.VMEM((1, gain_size // 2), F32),
            pltpu.VMEM((1, gain_size // 2), F32),
            pltpu.VMEM((gain_size // 128 + 8, 128), F32),
            pltpu.SemaphoreType.DMA((2 * (len(blocks) + PARTS) + 1,)),
            pltpu.SemaphoreType.DMA((3 * (len(blocks) + 1),)),
            pltpu.SemaphoreType.DMA((4, PARTS)),
            pltpu.SemaphoreType.DMA((4, PARTS)),
            pltpu.SemaphoreType.DMA((2,)),
            pltpu.SemaphoreType.DMA((2 * (width // LANES + 1) + 1,)),
        ],
        compiler_params=pltpu.CompilerParams(
            collective_id=0, has_side_effects=True, vmem_limit_bytes=56 * 2**20
        ),
    )(key_grads, router_grads, gain_grads, key_state, router_state, gain_state)


def on_device(
    wide_size,
    key_grads,
    router_grads,
    gain_grads,
    key_master,
    key_first,
    key_second,
    router_master,
    router_first,
    router_second,
    gain_master,
    gain_first,
    gain_second,
):
    key_state = [key_master, key_first, key_second]
    router_state = [router_master, router_first, router_second]
    gain_state = [x.reshape(1, -1) for x in (gain_master, gain_first, gain_second)]
    sums = reduce_grads(
        wide_size, key_grads, router_grads, gain_grads, key_state, router_state, gain_state
    )
    key_new, router_new, gain_new, key_weight, router_weight, gain_weight = update_all(
        *sums, key_state, router_state, gain_state
    )
    return (
        *key_new,
        *router_new,
        *[x.reshape(-1) for x in gain_new],
        key_weight.reshape(-1, key_weight.shape[2]),
        router_weight,
        gain_weight.reshape(-1),
    )


def solution(mesh):
    state = (P("narrow", None),) * 3 + (P(None, "narrow"),) * 3 + (P("narrow"),) * 3
    grads = (
        P("wide", "narrow", None, None, None),
        P("wide", "narrow", None, None, None),
        P("wide", "narrow", None, None),
    )
    return jax.shard_map(
        functools.partial(on_device, mesh.shape["wide"]),
        mesh=mesh,
        in_specs=grads + state,
        out_specs=state + (P(), P(), P()),
        check_vma=False,
    )
```

```python
import functools
import math

import jax
import jax.numpy as jnp
from jax import lax
from jax.experimental import pallas as pl
from jax.experimental.pallas import tpu as pltpu
from jax.sharding import PartitionSpec as P

beta_one = 0.9
beta_two = 0.95
step_rate = 0.01
epsilon = 1e-08
bias_one = 1.0 - 0.9**10
bias_two = 1.0 - 0.95**10

LANES = 128
PARTS = 6
HALVED_BITS = 4
F32, BF16 = jnp.float32, jnp.bfloat16


def adamw(master, first_moment, second, gradient, factor, decay_rate):
    scaled = factor * gradient
    first_new = beta_one * first_moment + (1.0 - beta_one) * scaled
    second_new = beta_two * second + (1.0 - beta_two) * scaled * scaled
    spread = second_new * (1.0 / bias_two)
    root = spread * lax.rsqrt(spread) + epsilon
    update = first_new * (1.0 / bias_one) / root
    if decay_rate:
        update = update + decay_rate * master
    return (master - step_rate * update, first_new, second_new)


def rows_loop(count, step, body):
    def one(i, carry):
        body(pl.multiple_of(i * step, 16))
        return carry

    lax.fori_loop(0, count // step, one, 0)


def layout(key_shape, router_shape):
    half_rows, half_cols = key_shape[0] // 2, router_shape[1] // 2
    blocks, at = [], 0
    for col in range(0, key_shape[1], LANES):
        blocks.append((at, half_rows, "key", col))
        at += half_rows
    for col in range(0, half_cols, LANES):
        blocks.append((at, router_shape[0], "router", col))
        at += router_shape[0]
    return blocks, at


def part_orders():
    return (
        ("x", 1, 2), (1, 2, "x"), (2, "x", 1),
        ("x", 2, 1), (1, "x", 2), (2, 1, "x"),
    )


def stage_shapes(part_rows, wide_bits):
    plans = []
    for order in part_orders():
        halves, count, plan = 2, part_rows, []
        for axis in (0,) + order + (3,):
            if axis == "x":
                halves = 1
            else:
                count //= 2
            plan.append((axis, (halves, count, LANES)))
        for axis in range(HALVED_BITS, wide_bits):
            plan.append((axis, (halves, count, LANES)))
        plans.append(plan)
    return plans


def reduce_kernel(
    plans,
    blocks,
    total_rows,
    clip_limit,
    key_ref,
    router_ref,
    gain_ref,
    key_state,
    router_state,
    gain_state,
    packed_out,
    small_out,
    grads,
    gain_grads,
    local,
    acc,
    full,
    gain_val,
    gain_in,
    square_val,
    square_in,
    send_bufs,
    recv_bufs,
    send_sem,
    recv_sem,
    gather_send,
    gather_recv,
    gain_send,
    gain_recv,
    square_send,
    square_recv,
    state,
    gain_mine,
    weight,
    far,
    gain_own,
    gain_new,
    gain_far,
    small,
    load_sem,
    state_sem,
    weight_send,
    weight_recv,
    gain_far_sem,
    out_sem,
):
    wide, narrow = lax.axis_index("wide"), lax.axis_index("narrow")
    stages = len(plans[0])
    part_rows = total_rows // PARTS
    wide_bits = stages - 1
    bit = [(wide // 2**k) % 2 for k in range(wide_bits)]

    def partner(axis):
        if axis == "x":
            return (wide, 1 - narrow)
        return (wide + (1 - 2 * bit[axis]) * 2**axis, narrow)

    diagonal = (partner(3)[0], 1 - narrow)
    friends = [partner(a) for a in ["x"] + list(range(wide_bits))] + [diagonal]
    barrier = pltpu.get_barrier_semaphore()
    for friend in friends:
        pl.semaphore_signal(barrier, inc=1, device_id=friend, device_id_type=pl.DeviceIdType.MESH)
    half_rows, half_cols = key_ref.shape[3] // 2, router_ref.shape[4] // 2
    gain_load = pltpu.make_async_copy(gain_ref.at[0, 0], gain_grads, load_sem.at[0])
    gain_load.start()
    loads = []
    for p in range(PARTS):
        part_loads = []
        for half in range(2):
            for at, count, kind, col in blocks:
                start, stop = max(at, p * part_rows), min(at + count, (p + 1) * part_rows)
                if start >= stop:
                    continue
                first = start - at + (half * half_rows if kind == "key" else 0)
                left = col + (half * half_cols if kind == "router" else 0)
                source = key_ref if kind == "key" else router_ref
                copy = pltpu.make_async_copy(
                    source.at[0, 0, :, pl.ds(first, stop - start), pl.ds(left, LANES)],
                    grads.at[:, half, pl.ds(start, stop - start), :],
                    load_sem.at[1 + len(part_loads) + sum(map(len, loads))],
                )
                copy.start()
                part_loads.append(copy)
        loads.append(part_loads)

    pl.semaphore_wait(barrier, len(friends))

    def remote(src, dst, send, recv, to):
        return pltpu.make_async_remote_copy(
            src_ref=src,
            dst_ref=dst,
            send_sem=send,
            recv_sem=recv,
            device_id=to,
            device_id_type=pl.DeviceIdType.MESH,
        )

    started = []
    gain_copies = []

    def send_gain(stage):
        copy = remote(
            gain_val.at[stage],
            gain_in.at[stage],
            gain_send.at[stage],
            gain_recv.at[stage],
            partner(plans[0][stage][0]),
        )
        copy.start()
        gain_copies.append(copy)

    gain_load.wait()
    gain_local = jnp.sum(gain_grads[...].astype(F32), axis=0, keepdims=True)
    gain_val[0] = gain_local.astype(BF16).astype(F32)
    send_gain(0)
    copies = []
    for p in range(PARTS):
        for load in loads[p]:
            load.wait()
        count = part_rows // 2
        sent = pl.multiple_of(p * part_rows + (1 - bit[0]) * count, 16)
        kept = pl.multiple_of(p * part_rows + bit[0] * count, 16)

        def fill(r, first):
            rows = pl.ds(pl.multiple_of(first + r, 16), 96)
            for half in range(2):
                local[half, rows, :] = grads[0, half, rows, :] + grads[1, half, rows, :]

        rows_loop(count, 96, functools.partial(fill, first=sent))
        copy = remote(
            local.at[:, pl.ds(sent, count), :],
            recv_bufs[p][0],
            send_sem.at[p, 0],
            recv_sem.at[p, 0],
            partner(0),
        )
        copy.start()
        copies.append(copy)
        started.append(copy)
        rows_loop(count, 96, functools.partial(fill, first=kept))

    state_loads = []

    def load_state(source, target):
        copy = pltpu.make_async_copy(source, target, state_sem.at[len(state_loads)])
        copy.start()
        state_loads.append(copy)

    base = [pl.multiple_of(p * part_rows + bit[0] * (part_rows // 2), 16) for p in range(PARTS)]
    rows_now = [part_rows // 2] * PARTS
    split = [False] * PARTS

    def add(p, stage, half, h, start, offset, r, step):
        previous = local if stage == 0 else acc
        mine = previous[half, pl.ds(pl.multiple_of(start + offset + r, 16), step), :]
        theirs = recv_bufs[p][stage][h, pl.ds(pl.multiple_of(offset + r, 16), step), :]
        return mine.astype(F32) + theirs.astype(F32)

    for stage in range(1, stages):
        if stage == 2:
            for i in range(3):
                load_state(gain_state[i], gain_mine.at[i])
                for at, count, kind, col in blocks:
                    source = key_state[i] if kind == "key" else router_state[i]
                    load_state(source.at[:, pl.ds(col, LANES)], state.at[i, pl.ds(at, count), :])
        gain_copies[stage - 1].wait_recv()
        gain_val[stage] = gain_val[stage - 1] + gain_in[stage - 1]
        send_gain(stage)
        fresh, pending = [], []
        for p in range(PARTS):
            axis, shape = plans[p][stage]
            copies[p].wait_recv()
            halves = [(narrow, 0)] if split[p] else [(0, 0), (1, 1)]
            send_buf = send_bufs[p][stage - 1]
            step = min(96, shape[1])
            if axis == "x":
                send_sets, keep_sets = [(1 - narrow, 1 - narrow, 0)], [(narrow, narrow)]
                send_offset = keep_offset = 0
            elif axis < HALVED_BITS:
                send_sets = [(half, h, h) for half, h in halves]
                keep_sets = halves
                send_offset = (1 - bit[axis]) * shape[1]
                keep_offset = bit[axis] * shape[1]
            else:
                send_sets, keep_sets = [(narrow, 0, 0)], []
                send_offset = keep_offset = 0

            def out(r, p=p):
                for half, h, slot in send_sets:
                    value = add(p, stage - 1, half, h, base[p], send_offset, r, step)
                    send_buf[slot, pl.ds(r, step), :] = value.astype(BF16)
                    if not keep_sets:
                        rows = pl.ds(pl.multiple_of(base[p] + r, 16), step)
                        acc[half, rows, :] = value.astype(BF16).astype(F32)

            rows_loop(shape[1], step, out)
            copy = remote(
                send_buf,
                recv_bufs[p][stage],
                send_sem.at[p, stage],
                recv_sem.at[p, stage],
                partner(axis),
            )
            copy.start()
            fresh.append(copy)
            started.append(copy)

            def keep(
                r, p=p, sets=keep_sets, start=base[p], offset=keep_offset, step=step
            ):
                for half, h in sets:
                    value = add(p, stage - 1, half, h, start, offset, r, step)
                    rows = pl.ds(pl.multiple_of(start + offset + r, 16), step)
                    acc[half, rows, :] = value

            if keep_sets:
                pending.append((shape[1], step, keep))
            if axis == "x":
                split[p] = True
            base[p] = pl.multiple_of(base[p] + keep_offset, 16)
            rows_now[p] = shape[1]
            if p % 3 == 2:
                for job in pending:
                    rows_loop(*job)
                pending = []
        copies = fresh

    gather_axes = [
        [3] + [a for a in reversed(part_orders()[p]) if a != "x"] + [0] for p in range(PARTS)
    ]
    gathers = []

    def gather(p, stage):
        rows = pl.ds(base[p], rows_now[p])
        axis = gather_axes[p][stage]
        copy = remote(
            full.at[rows, :],
            full.at[rows, :],
            gather_send.at[p, stage],
            gather_recv.at[p, stage],
            partner(axis),
        )
        copy.start()
        started.append(copy)
        base[p] = pl.multiple_of(base[p] - bit[axis] * rows_now[p], 16)
        rows_now[p] = 2 * rows_now[p]
        return copy

    squares = jnp.zeros((8, LANES), F32)
    for p in range(PARTS):
        copies[p].wait_recv()
        count = rows_now[p]
        value = add(p, stages - 1, narrow, 0, base[p], 0, 0, count)
        full[pl.ds(base[p], count), :] = value.astype(BF16)
        gathers.append(gather(p, 0))
        squares = squares + jnp.sum((value * value).reshape(count // 8, 8, LANES), axis=0)

    def send_square(source, slot, to):
        copy = remote(
            square_val.at[source],
            square_in.at[slot],
            square_send.at[slot],
            square_recv.at[slot],
            to,
        )
        copy.start()
        started.append(copy)
        return copy

    square_val[0] = squares
    square_copies = [
        send_square(0, 0, partner("x")),
        send_square(0, 1, partner(3)),
        send_square(0, 2, diagonal),
    ]
    gain_copies[stages - 1].wait_recv()
    gain_sum = gain_val[stages - 1] + gain_in[stages - 1]
    gain_val[stages] = gain_sum
    left = pl.multiple_of(narrow * gain_own.shape[1], 128)
    gain_own[...] = gain_val[stages, :, pl.ds(left, gain_own.shape[1])]
    for copy in square_copies:
        copy.wait_recv()
    square_val[1] = (square_val[0] + square_in[0]) + (square_in[1] + square_in[2])
    square_copy = send_square(1, 3, partner(2))
    for p in range(PARTS):
        gathers[p].wait_recv()
        gathers[p] = gather(p, 1)
    for stage in range(2, 4):
        square_copy.wait_recv()
        square_val[stage] = square_val[stage - 1] + square_in[stage + 1]
        square_copy = send_square(stage, stage + 2, partner((1, 0)[stage - 2]))
    for copy in state_loads:
        copy.wait()
    square_copy.wait_recv()
    total = jnp.sum(square_val[3] + square_in[5]) + jnp.sum(gain_sum * gain_sum)
    total = jnp.full((8, 128), total, F32)
    gain_tiles = gain_own.shape[1] // 128
    small[2 * gain_tiles :, :] = clip_limit / jnp.maximum(jnp.sqrt(total), clip_limit)
    factor = small[2 * gain_tiles : 2 * gain_tiles + 1, 0:1]

    def forward(p, hop, start, axis):
        block = far.at[pl.ds(start, quarter_rows), :]
        copy = remote(block, block, weight_send.at[hop, p], weight_recv.at[hop, p], partner(axis))
        copy.start()
        started.append(copy)
        return copy

    quarter_rows = part_rows // 4
    held, across = [], []
    for p in range(PARTS):
        gathers[p].wait_recv()
        start = base[p]
        held.append(start)
        gathers[p] = gather(p, 2)

        def renew(r, p=p, start=start):
            rows = pl.ds(pl.multiple_of(start + r, 16), 64)
            old = [state[i, rows, :] for i in range(3)]
            new = adamw(*old, full[rows, :].astype(F32), factor, 0.1)[0]
            weight[p, pl.ds(r, 64), :] = new.astype(BF16)

        rows_loop(quarter_rows, 64, renew)
        copy = remote(
            weight.at[p],
            far.at[pl.ds(start, quarter_rows), :],
            weight_send.at[0, p],
            weight_recv.at[0, p],
            partner("x"),
        )
        copy.start()
        started.append(copy)
        across.append(copy)
    gain_new[...] = adamw(
        gain_mine[0], gain_mine[1], gain_mine[2], gain_own[...], factor, 0.0
    )[0]
    gain_copy = remote(gain_new, gain_far, gain_far_sem.at[0], gain_far_sem.at[1], partner("x"))
    gain_copy.start()

    beside, own, other = [], [], []
    for p in range(PARTS):
        gathers[p].wait_recv()
        gathers[p] = gather(p, 3)
        across[p].wait_recv()
        beside.append(forward(p, 1, held[p], gather_axes[p][2]))
        own.append(forward(p, 2, held[p], 0))
    for p in range(PARTS):
        beside[p].wait_recv()
        step = (1 - 2 * bit[gather_axes[p][2]]) * quarter_rows
        other.append(forward(p, 3, pl.multiple_of(held[p] + step, 16), 0))

    out_copies = []

    def leave(source, target):
        copy = pltpu.make_async_copy(source, target, out_sem.at[len(out_copies)])
        copy.start()
        out_copies.append(copy)

    def leave_packed(source, place):
        keys = [at for at, _, kind, _ in blocks if kind == "key"]
        for i, at in enumerate(keys):
            leave(source.at[pl.ds(at, half_rows), :], packed_out.at[place, i])
        at = len(keys) * half_rows
        rest = total_rows - at
        leave(
            source.at[pl.ds(at, rest), :], packed_out.at[place, len(keys), pl.ds(0, rest), :]
        )

    for copy in gathers:
        copy.wait_recv()
    leave_packed(full, 0)
    gain_copy.wait_recv()
    for j in range(gain_tiles):
        cols = slice(128 * j, 128 * (j + 1))
        small[j : j + 1, :] = gain_own[:, cols]
        small[gain_tiles + j : gain_tiles + j + 1, :] = gain_far[:, cols]
    leave(small, small_out.at[pl.ds(0, small.shape[0]), :])
    for copy in own + other:
        copy.wait_recv()
    leave_packed(far, 1)
    for copy in started + gain_copies + [gain_copy]:
        copy.wait_send()
    for copy in out_copies:
        copy.wait()


def update_kernel(
    packed,
    small_in,
    key_state,
    router_state,
    gain_state,
    key_new,
    router_new,
    gain_new,
    key_weight,
    router_weight,
    gain_weight,
    keys,
    routers,
    small,
    gain_rows,
    key_sem,
    other_sem,
):
    narrow, at = lax.axis_index("narrow"), pl.program_id(0)
    steps = pl.num_programs(0)
    blocks, block_rows, experts = keys.shape[1], key_new[0].shape[0], router_new[0].shape[0]
    gain_tiles = gain_rows.shape[0] // 2

    def key_copy(i):
        rows = pl.ds(pl.multiple_of(i * block_rows, 16), block_rows)
        return pltpu.make_async_copy(
            packed.at[:, pl.ds(0, blocks), rows, :], keys.at[:, :, rows, :], key_sem.at[i]
        )

    other_copies = [
        pltpu.make_async_copy(
            small_in.at[pl.ds(0, small.shape[0]), :], small, other_sem.at[0]
        ),
        pltpu.make_async_copy(
            packed.at[:, blocks, pl.ds(0, routers.shape[1]), :], routers, other_sem.at[1]
        ),
    ]

    @pl.when(at == 0)
    def _():
        for copy in other_copies:
            copy.start()
        for i in range(keys.shape[2] // block_rows):
            key_copy(i).start()
        for copy in other_copies:
            copy.wait()

    factor = small[2 * gain_tiles : 2 * gain_tiles + 1, 0:1]

    def update(state, gradient, decay_rate, new, rows, cols):
        old = [ref[rows, cols] for ref in state]
        values = adamw(*old, gradient.astype(F32), factor, decay_rate)
        for ref, value in zip(new, values):
            ref[rows, cols] = value
        return values[0]

    @pl.when(at == 0)
    def _():
        for j in range(gain_tiles):
            cols = slice(128 * j, 128 * (j + 1))
            value = update(
                gain_state, small[j : j + 1, :], 0.0, gain_new, slice(0, 1), cols
            )
            gain_rows[pl.ds(narrow * gain_tiles + j, 1), :] = value
            other = small[gain_tiles + j : gain_tiles + j + 1, :]
            gain_rows[pl.ds((1 - narrow) * gain_tiles + j, 1), :] = other
        gain_weight[...] = gain_rows[...].astype(BF16)

    rows = pl.ds(pl.multiple_of(at * experts, 16), experts)
    value = update(
        router_state, routers[0, rows, :], 0.1, router_new, slice(None), slice(None)
    )

    def columns(n):
        return pl.ds(pl.multiple_of((n * steps + at) * LANES, 128), LANES)

    router_weight[:, columns(narrow)] = value.astype(BF16)
    router_weight[:, columns(1 - narrow)] = routers[1, rows, :]

    key_copy(at).wait()
    rows = pl.ds(pl.multiple_of(at * block_rows, 16), block_rows)
    for j in range(blocks):
        cols = slice(LANES * j, LANES * (j + 1))
        value = update(key_state, keys[0, j, rows, :], 0.1, key_new, slice(None), cols)
        key_weight[narrow, :, cols] = value.astype(BF16)
        key_weight[1 - narrow, :, cols] = keys[1, j, rows, :]


def update_all(packed, small, key_state, router_state, gain_state):
    (rows, width), (experts, cols) = key_state[0].shape, router_state[0].shape
    gain = gain_state[0].shape[1]
    steps = cols // LANES
    key_spec = pl.BlockSpec((rows // steps, width), lambda i: (i, 0))
    router_spec = pl.BlockSpec((experts, LANES), lambda i: (0, i))
    gain_spec = pl.BlockSpec((1, gain), lambda i: (0, 0))
    shape = jax.ShapeDtypeStruct
    return pl.pallas_call(
        update_kernel,
        grid=(steps,),
        out_shape=(
            [shape((rows, width), F32)] * 3,
            [shape((experts, cols), F32)] * 3,
            [shape((1, gain), F32)] * 3,
            shape((2, rows, width), BF16),
            shape((experts, 2 * cols), BF16),
            shape((2 * gain // 128, 128), BF16),
        ),
        in_specs=[pl.BlockSpec(memory_space=pltpu.HBM)] * 2
        + [[key_spec] * 3, [router_spec] * 3, [gain_spec] * 3],
        out_specs=(
            [key_spec] * 3,
            [router_spec] * 3,
            [gain_spec] * 3,
            pl.BlockSpec((2, rows // steps, width), lambda i: (0, i, 0)),
            pl.BlockSpec((experts, 2 * cols), lambda i: (0, 0)),
            pl.BlockSpec((2 * gain // 128, 128), lambda i: (0, 0)),
        ),
        scratch_shapes=[
            pltpu.VMEM((2, width // LANES, rows, LANES), BF16),
            pltpu.VMEM((2, experts * steps, LANES), BF16),
            pltpu.VMEM((2 * gain // 128 + 8, 128), F32),
            pltpu.VMEM((2 * gain // 128, 128), F32),
            pltpu.SemaphoreType.DMA((steps,)),
            pltpu.SemaphoreType.DMA((2,)),
        ],
        compiler_params=pltpu.CompilerParams(vmem_limit_bytes=46 * 2**20),
    )(packed, small, key_state, router_state, gain_state)


def reduce_grads(
    wide_size, key_grads, router_grads, gain_grads, key_state, router_state, gain_state
):
    key_shape, router_shape = key_grads.shape[3:], router_grads.shape[3:]
    gain_size = gain_grads.shape[3]
    blocks, total_rows = layout(key_shape, router_shape)
    wide_bits = wide_size.bit_length() - 1
    plans = stage_shapes(total_rows // PARTS, wide_bits)
    stages = len(plans[0])
    count = math.prod(key_shape) + math.prod(router_shape) + gain_size
    hbm = pl.BlockSpec(memory_space=pl.ANY)
    half_rows, width = key_shape[0] // 2, key_shape[1]
    return pl.pallas_call(
        functools.partial(
            reduce_kernel, plans, blocks, total_rows, 0.5 * math.sqrt(count)
        ),
        out_shape=(
            jax.ShapeDtypeStruct((2, 4 * (width // LANES), half_rows, LANES), BF16),
            jax.ShapeDtypeStruct((16 * half_rows, 128), F32),
        ),
        in_specs=[hbm] * 3 + [[hbm] * 3] * 3,
        out_specs=(hbm, hbm),
        scratch_shapes=[
            pltpu.VMEM((2, 2, total_rows, LANES), BF16),
            pltpu.VMEM((2, gain_size), BF16),
            pltpu.VMEM((2, total_rows, LANES), BF16),
            pltpu.VMEM((2, total_rows, LANES), F32),
            pltpu.VMEM((total_rows, LANES), BF16),
            pltpu.VMEM((stages + 1, 1, gain_size), F32),
            pltpu.VMEM((stages, 1, gain_size), F32),
            pltpu.VMEM((5, 8, LANES), F32),
            pltpu.VMEM((6, 8, LANES), F32),
            [[pltpu.VMEM(shape, BF16) for _, shape in plan[1:]] for plan in plans],
            [[pltpu.VMEM(shape, BF16) for _, shape in plan] for plan in plans],
            pltpu.SemaphoreType.DMA((PARTS, stages)),
            pltpu.SemaphoreType.DMA((PARTS, stages)),
            pltpu.SemaphoreType.DMA((PARTS, 4)),
            pltpu.SemaphoreType.DMA((PARTS, 4)),
            pltpu.SemaphoreType.DMA((stages,)),
            pltpu.SemaphoreType.DMA((stages,)),
            pltpu.SemaphoreType.DMA((6,)),
            pltpu.SemaphoreType.DMA((6,)),
            pltpu.VMEM((3, total_rows, LANES), F32),
            pltpu.VMEM((3, 1, gain_size // 2), F32),
            pltpu.VMEM((PARTS, total_rows // PARTS // 4, LANES), BF16),
            pltpu.VMEM((total_rows, LANES), BF16),
            pltpu.VMEM((1, gain_size // 2), F32),
            pltpu.VMEM((1, gain_size // 2), F32),
            pltpu.VMEM((1, gain_size // 2), F32),
            pltpu.VMEM((gain_size // 128 + 8, 128), F32),
            pltpu.SemaphoreType.DMA((2 * (len(blocks) + PARTS) + 1,)),
            pltpu.SemaphoreType.DMA((3 * (len(blocks) + 1),)),
            pltpu.SemaphoreType.DMA((4, PARTS)),
            pltpu.SemaphoreType.DMA((4, PARTS)),
            pltpu.SemaphoreType.DMA((2,)),
            pltpu.SemaphoreType.DMA((2 * (width // LANES + 1) + 1,)),
        ],
        compiler_params=pltpu.CompilerParams(
            collective_id=0, has_side_effects=True, vmem_limit_bytes=56 * 2**20
        ),
    )(key_grads, router_grads, gain_grads, key_state, router_state, gain_state)


def on_device(
    wide_size,
    key_grads,
    router_grads,
    gain_grads,
    key_master,
    key_first,
    key_second,
    router_master,
    router_first,
    router_second,
    gain_master,
    gain_first,
    gain_second,
):
    key_state = [key_master, key_first, key_second]
    router_state = [router_master, router_first, router_second]
    gain_state = [x.reshape(1, -1) for x in (gain_master, gain_first, gain_second)]
    sums = reduce_grads(
        wide_size, key_grads, router_grads, gain_grads, key_state, router_state, gain_state
    )
    key_new, router_new, gain_new, key_weight, router_weight, gain_weight = update_all(
        *sums, key_state, router_state, gain_state
    )
    return (
        *key_new,
        *router_new,
        *[x.reshape(-1) for x in gain_new],
        key_weight.reshape(-1, key_weight.shape[2]),
        router_weight,
        gain_weight.reshape(-1),
    )


def solution(mesh):
    state = (P("narrow", None),) * 3 + (P(None, "narrow"),) * 3 + (P("narrow"),) * 3
    grads = (
        P("wide", "narrow", None, None, None),
        P("wide", "narrow", None, None, None),
        P("wide", "narrow", None, None),
    )
    return jax.shard_map(
        functools.partial(on_device, mesh.shape["wide"]),
        mesh=mesh,
        in_specs=grads + state,
        out_specs=state + (P(), P(), P()),
        check_vma=False,
    )
```
